32 devices in a mesh: seq: 8 (over y, x, core), enc: 4 (over z).
Axes of the slice: x: 2, y: 2, z: 4, core: 2. Of those that a mesh axis runs over, the one named last changes fastest.
Arguments:
- queries: bfloat16 [1024, 8192], P('seq', 'enc'), may hold values from -63 to 63
- image_key_value: bfloat16 [2, 32, 1601, 1024], P(None, ('seq', 'enc')), may hold values from -16 to 16
- image_spans: int32 [8, 2], replicated, may hold values from 0 to 1024, as said below
- tile_counts: int32 [8], replicated, may hold values from 1 to 4
- cross_gate: float32 [1], replicated, may hold values from 0.2 to 2
- grad_out: bfloat16 [1024, 8192], P('seq', 'enc'), may hold values from -6 to 6
Outputs:
- attended: bfloat16 [1024, 8192], P('seq', 'enc')
- grad_queries: bfloat16 [1024, 8192], P('seq', 'enc')
- grad_image_kv: bfloat16 [2, 32, 1601, 1024], P(None, ('seq', 'enc'))
The draws below stay inside these ranges and needn't reach their ends.
Inputs may be any that keep to these rules, and one draw needn't show every extreme that they name: `image_spans`: image m owns tiles 4 m to 4 m + 3. Its span starts in text shard m (positions (m) * 128 to (m) * 128 + 127), starts do not fall from one image to the next within a shard, and each span holds 1 to 128 positions.
All inputs are finite; a program needn't handle non-finite values.
Results may differ from the reference program's by a relative error of at most 0.0062.
Values may be sent and summed in bfloat16 or wider, within the bound.
No kernel may reach another device: no remote copies, remote signals or barrier semaphores. Data moves between devices by JAX's collectives and lax.ppermute only.
A program may use at most 128 MiB of HBM per device.

```python
import jax
import jax.numpy as jnp
from jax import lax

QUERY_HEAD_COUNT = 64
KEY_VALUE_HEADS = 8
HEAD_SIZE = 128
TOKENS_PER_TILE = 1601
TILES = 4
TEXT_PER_SHARD = 128
TEXT = 1024
TILE_COUNT = 32
NIMG = 8
IMG_ROW = 1
N_SEQ = 8
N_ENC = 4


def span_table(key):
    base = jax.random.fold_in(key, 101)
    start_key, length_key = jax.random.split(base)
    offsets = jax.random.randint(start_key, (NIMG,), 0, TEXT_PER_SHARD)
    offsets = jnp.sort(offsets.reshape(NIMG // IMG_ROW, IMG_ROW), axis=1).reshape(NIMG)
    row_ids = jnp.arange(NIMG, dtype=jnp.int32) // IMG_ROW
    starts = row_ids * TEXT_PER_SHARD + offsets
    starts = starts.at[0].set(0)
    lengths = jax.random.randint(length_key, (NIMG,), 1, TEXT_PER_SHARD + 1)
    lengths = lengths.at[1].set(TEXT_PER_SHARD)
    span_ends = jnp.minimum(starts + lengths, TEXT)
    span_ends = span_ends.at[NIMG - 1].set(TEXT)
    return jnp.stack([starts, span_ends], 1).astype(jnp.int32)


def draw_image_spans(key, part):
    return span_table(key)


def draw_tile_counts(key, part):
    counts = jax.random.randint(jax.random.fold_in(key, 202), (NIMG,), 1, TILES + 1)
    return counts.at[0].set(TILES).astype(jnp.int32)


def draw_queries(key, part):
    base = jax.random.fold_in(key, 303)
    values = 2.0 * jnp.clip(jax.random.normal(base, (TEXT, QUERY_HEAD_COUNT * HEAD_SIZE), jnp.float32), -4.0, 4.0)
    return values.astype(jnp.bfloat16)


def draw_image_key_value(key, part):
    leading_key, trailing_key = jax.random.split(jax.random.fold_in(key, 404))
    key_portion = jnp.clip(jax.random.normal(leading_key, (TILE_COUNT, TOKENS_PER_TILE, KEY_VALUE_HEADS * HEAD_SIZE), jnp.float32), -4.0, 4.0)
    value_portion = 4.0 * jnp.clip(jax.random.normal(trailing_key, (TILE_COUNT, TOKENS_PER_TILE, KEY_VALUE_HEADS * HEAD_SIZE), jnp.float32), -4.0, 4.0)
    return jnp.stack([key_portion, value_portion], 0).astype(jnp.bfloat16)


def level_of(own_key, shape, pieces, least, high):
    def one(axis_at, blocks):
        draws = jax.random.uniform(jax.random.fold_in(jax.random.fold_in(own_key, 6), axis_at), (blocks,), jnp.float32, least / len(pieces), high / len(pieces))
        return jnp.repeat(jnp.exp(draws), shape[axis_at] // blocks).reshape((-1,) + (1,) * (len(shape) - axis_at - 1))

    loudness = one(*pieces[0])
    for cut in pieces[1:]:
        loudness = loudness * one(*cut)
    return loudness


def bell_draw(stream_key, extent, spread, most, cuts=(), held_as=jnp.bfloat16):
    entries = jax.random.normal(stream_key, extent, jnp.float32) * spread
    if len(cuts) > 0:
        entries = level_of(stream_key, extent, cuts, -0.22, 0.18) * entries
    return jnp.clip(entries, min=-most, max=most).astype(held_as)


def setup_inputs(seed: int = 0) -> dict:
    key_of = jax.random.split(jax.random.key(seed), 7)
    return {
        "queries": draw_queries(jax.random.fold_in(key_of[6], 71), 0),
        "image_key_value": draw_image_key_value(jax.random.fold_in(key_of[6], 71), 0),
        "image_spans": draw_image_spans(jax.random.fold_in(key_of[6], 71), 0),
        "tile_counts": draw_tile_counts(jax.random.fold_in(key_of[6], 71), 0),
        "cross_gate": jnp.clip(jax.random.uniform(key_of[4], (1,), jnp.float32, 0.2, 2.0), 0.2, 2.0),
        "grad_out": bell_draw(key_of[5], (TEXT, QUERY_HEAD_COUNT * HEAD_SIZE), 1.0, 6.0, ((0, 8), (1, 4))),
    }


NEG_FILL = -1.0e30


def visible_rows(image_spans, tile_counts, first_tile, tile_total, first_text, text_rows):
    image_total = image_spans.shape[0]
    tile_ids = first_tile + jnp.arange(tile_total, dtype=jnp.int32)
    image_ids = jnp.floor_divide(tile_ids, TILES)
    slot_ids = tile_ids - image_ids * TILES
    lookup = (image_ids[:, None] == jnp.arange(image_total, dtype=jnp.int32)[None, :]).astype(jnp.int32)
    starts = jnp.sum(lookup * image_spans[:, 0][None, :], axis=1)
    span_ends = jnp.sum(lookup * image_spans[:, 1][None, :], axis=1)
    in_use = jnp.sum(lookup * tile_counts[None, :], axis=1)
    usable = (tile_ids >= 0) & (slot_ids < in_use)
    positions = first_text + jnp.arange(text_rows, dtype=jnp.int32)
    return usable[None, :] & (positions[:, None] >= starts[None, :]) & (positions[:, None] < span_ends[None, :])


def head_terms(query_head, grad_head, key_head, value_head, visible, softmax_scale):
    query_wide = query_head.astype(jnp.float32)
    grad_wide = grad_head.astype(jnp.float32)
    key_wide = key_head.astype(jnp.float32)
    value_wide = value_head.astype(jnp.float32)
    text_rows = query_head.shape[0]
    head_groups = query_head.shape[1]
    head_dim = query_head.shape[2]
    tile_total = visible.shape[1]
    scores = jnp.einsum("tgd,jd->tgj", query_wide, key_wide) * softmax_scale
    tile_scores = jnp.moveaxis(scores.reshape(text_rows, head_groups, tile_total, TOKENS_PER_TILE), 2, 0)
    tile_values = value_wide.reshape(tile_total, TOKENS_PER_TILE, head_dim)

    def online(carried, item):
        tile_score, column, value_tile = item
        run_max, run_total, run_out = carried
        tile_mask = column[:, None, None]
        tile_max = jnp.max(jnp.where(tile_mask, tile_score, NEG_FILL), axis=2)
        new_max = jnp.maximum(run_max, tile_max)
        factor = jnp.exp(run_max - new_max)
        probs = jnp.where(tile_mask, jnp.exp(tile_score - new_max[:, :, None]), 0.0)
        probs_low = lax.optimization_barrier(probs.astype(jnp.bfloat16)).astype(jnp.float32)
        new_total = run_total * factor + jnp.sum(probs, axis=2)
        new_out = run_out * factor[:, :, None] + jnp.einsum("tgj,jd->tgd", probs_low, value_tile)
        return (new_max, new_total, new_out), None

    starting_state = (jnp.full((text_rows, head_groups), NEG_FILL, jnp.float32), jnp.zeros((text_rows, head_groups), jnp.float32),
               jnp.zeros((text_rows, head_groups, head_dim), jnp.float32))
    (run_max, run_total, run_out), unused = lax.scan(online, starting_state, (tile_scores, visible.T, tile_values))
    seen = run_total > 0.0
    safe_total = jnp.where(seen, run_total, 1.0)
    log_total = jnp.where(seen, run_max + jnp.log(safe_total), 0.0)
    mixed = jnp.where(seen[:, :, None], run_out / safe_total[:, :, None], 0.0)
    row_mask = jnp.repeat(visible, TOKENS_PER_TILE, axis=1)
    wide_mask = row_mask[:, None, :]
    weights = jnp.where(wide_mask, jnp.exp(scores - log_total[:, :, None]), 0.0)
    weights_low = lax.optimization_barrier(weights.astype(jnp.bfloat16)).astype(jnp.float32)
    row_delta = jnp.sum(grad_wide * mixed, axis=2)
    grad_weights = jnp.einsum("tgd,jd->tgj", grad_wide, value_wide)
    grad_scores = lax.optimization_barrier((weights * (grad_weights - row_delta[:, :, None])).astype(jnp.bfloat16)).astype(jnp.float32)
    query_grad = jnp.einsum("tgj,jd->tgd", grad_scores, key_wide) * softmax_scale
    key_grad = (jnp.einsum("tgj,tgd->jd", grad_scores, query_wide) * softmax_scale).astype(jnp.bfloat16)
    value_grad = jnp.einsum("tgj,tgd->jd", weights_low, grad_wide).astype(jnp.bfloat16)
    return mixed, query_grad, key_grad, value_grad


def reference(queries, image_key_value, image_spans, tile_counts, cross_gate, grad_out):
    softmax_scale = HEAD_SIZE ** -0.5
    head_groups = QUERY_HEAD_COUNT // KEY_VALUE_HEADS
    tile_row_block = N_ENC * TOKENS_PER_TILE
    gate_value = jnp.tanh(cross_gate[0])
    gradient_blended = (gate_value * grad_out.astype(jnp.float32)).astype(jnp.bfloat16)
    key_row_block = image_key_value[0].reshape(N_SEQ, tile_row_block, KEY_VALUE_HEADS, HEAD_SIZE)
    value_row_block = image_key_value[1].reshape(N_SEQ, tile_row_block, KEY_VALUE_HEADS, HEAD_SIZE)
    query_row_block = queries.reshape(N_SEQ, TEXT_PER_SHARD, KEY_VALUE_HEADS, head_groups, HEAD_SIZE)
    gradient_row_block = gradient_blended.reshape(N_SEQ, TEXT_PER_SHARD, KEY_VALUE_HEADS, head_groups, HEAD_SIZE)

    def row_step(carried, row_index):
        earlier = jnp.maximum(row_index - 1, 0)
        reach_keys = jnp.concatenate([key_row_block[earlier], key_row_block[row_index]], 0)
        reach_values = jnp.concatenate([value_row_block[earlier], value_row_block[row_index]], 0)
        visible = visible_rows(image_spans, tile_counts, (row_index - 1) * N_ENC, 2 * N_ENC, row_index * TEXT_PER_SHARD, TEXT_PER_SHARD)

        def one_head(head_items):
            query_head, grad_head, key_head, value_head = head_items
            return head_terms(query_head, grad_head, key_head, value_head, visible, softmax_scale)

        mixed, query_grad, key_grad, value_grad = lax.map(
            one_head,
            (jnp.moveaxis(query_row_block[row_index], 1, 0), jnp.moveaxis(gradient_row_block[row_index], 1, 0),
             jnp.moveaxis(reach_keys, 1, 0), jnp.moveaxis(reach_values, 1, 0)))
        finished_keys = (carried[0].astype(jnp.float32) + key_grad[:, :tile_row_block].astype(jnp.float32)).astype(jnp.bfloat16)
        finished_values = (carried[1].astype(jnp.float32) + value_grad[:, :tile_row_block].astype(jnp.float32)).astype(jnp.bfloat16)
        attended_rows = (gate_value * mixed).astype(jnp.bfloat16)
        return (key_grad[:, tile_row_block:], value_grad[:, tile_row_block:]), (attended_rows, query_grad.astype(jnp.bfloat16), finished_keys, finished_values)

    starting_state = (jnp.zeros((KEY_VALUE_HEADS, tile_row_block, HEAD_SIZE), jnp.bfloat16), jnp.zeros((KEY_VALUE_HEADS, tile_row_block, HEAD_SIZE), jnp.bfloat16))
    last_rows, stacked = lax.scan(row_step, starting_state, jnp.arange(N_SEQ, dtype=jnp.int32))
    attended = jnp.transpose(stacked[0], (0, 2, 1, 3, 4)).reshape(N_SEQ * TEXT_PER_SHARD, QUERY_HEAD_COUNT * HEAD_SIZE)
    grad_queries = jnp.transpose(stacked[1], (0, 2, 1, 3, 4)).reshape(N_SEQ * TEXT_PER_SHARD, QUERY_HEAD_COUNT * HEAD_SIZE)

    def assemble(shifted, final_row):
        entire_result = jnp.concatenate([shifted[1:], final_row[None]], 0)
        entire_result = entire_result.reshape(N_SEQ, KEY_VALUE_HEADS, N_ENC, TOKENS_PER_TILE, HEAD_SIZE)
        return jnp.transpose(entire_result, (0, 2, 3, 1, 4)).reshape(N_SEQ * N_ENC, TOKENS_PER_TILE, KEY_VALUE_HEADS * HEAD_SIZE)

    grad_image_kv = jnp.stack([assemble(stacked[2], last_rows[0]), assemble(stacked[3], last_rows[1])], 0)
    return attended, grad_queries, grad_image_kv
```

```python
import functools

import jax
import jax.numpy as jnp
from jax import lax
from jax.experimental import pallas as pl
from jax.experimental.pallas import tpu as pltpu
from jax.sharding import PartitionSpec as P

HEAD_SIZE = 128
TILES = 4
LOW = -1e30
HIGH = 1e30
SCALE = HEAD_SIZE ** (-0.5)
LOG2E = 1.4426950408889634
BLOCK = 512
ROW_PAD = 16


def rotated(x, axis, by):
    total = lax.axis_size(axis)
    return lax.ppermute(x, axis, [(i, (i + by) % total) for i in range(total)])


def shifted(x, axis, by):
    total = lax.axis_size(axis)
    return lax.ppermute(x, axis, [(i, i + by) for i in range(total) if 0 <= i + by < total])


def dot_nt(a, b):
    return lax.dot_general(a, b, (((1,), (1,)), ((), ())), preferred_element_type=jnp.float32)


def dot_tn(a, b):
    return lax.dot_general(a, b, (((0,), (0,)), ((), ())), preferred_element_type=jnp.float32)


def dot_nn(a, b):
    return lax.dot_general(a, b, (((1,), (0,)), ((), ())), preferred_element_type=jnp.float32)


def stacked(ref, groups):
    return jnp.concatenate(
        [ref[0, :, i * HEAD_SIZE : (i + 1) * HEAD_SIZE] for i in range(groups)], axis=0
    )


def cuts(tokens, padded):
    whole = tokens // BLOCK
    parts = [(i * BLOCK, BLOCK, BLOCK) for i in range(whole)]
    if padded > whole * BLOCK:
        parts.append((whole * BLOCK, padded - whole * BLOCK, tokens - whole * BLOCK))
    return parts


def row_fill(values, valid, fill):
    if values.shape[0] == valid:
        return values
    rows = lax.broadcasted_iota(jnp.int32, values.shape, 0)
    return jnp.where(rows < valid, values, fill)


def forward_kernel(tokens, groups, at_ref, q_ref, g_ref, k_ref, v_ref, o_ref, lse_ref, delta_ref, s_ref):
    padded = k_ref.shape[2]
    parts = cuts(tokens, padded)
    q = stacked(q_ref, groups)
    top = None
    for start, size, valid in parts:
        s = dot_nt(k_ref[0, 0, start : start + size], q)
        s = row_fill(s, valid, LOW)
        s_ref[start : start + size] = s
        peak = jnp.max(s, axis=0, keepdims=True)
        top = peak if top is None else jnp.maximum(top, peak)
    top = top * (SCALE * LOG2E)
    total = None
    out = None
    for start, size, valid in parts:
        p = jnp.exp2(s_ref[start : start + size] * (SCALE * LOG2E) - top)
        part_total = jnp.sum(p, axis=0, keepdims=True)
        part_out = dot_tn(v_ref[0, 0, start : start + size], p.astype(jnp.bfloat16))
        total = part_total if total is None else total + part_total
        out = part_out if out is None else out + part_out
    out = out / total
    lse = top + jnp.log2(total)
    o_ref[0] = out
    for i in range(groups):
        span = slice(i * HEAD_SIZE, (i + 1) * HEAD_SIZE)
        g_t = g_ref[0, :, span].astype(jnp.float32).T
        lse_ref[0, i : i + 1] = lse[:, span]
        delta_ref[0, i : i + 1] = jnp.sum(g_t * out[:, span], axis=0, keepdims=True)


def backward_kernel(
    tokens,
    groups,
    first,
    at_ref,
    q_ref,
    g_ref,
    k_ref,
    v_ref,
    o_ref,
    lse_ref,
    delta_ref,
    weight_ref,
    *rest,
):
    if first:
        old_ref, mix_ref, dq_ref, dkv_ref = rest
        mix_in_ref = dq_in_ref = None
    else:
        mix_in_ref, dq_in_ref, old_ref, mix_ref, dq_ref, dkv_ref = rest
    padded = k_ref.shape[2]
    q = stacked(q_ref, groups)
    g = stacked(g_ref, groups)
    lse = jnp.concatenate([lse_ref[0, i : i + 1] for i in range(groups)], axis=1)
    delta = jnp.concatenate([delta_ref[0, i : i + 1] for i in range(groups)], axis=1)
    grad_q = None
    for start, size, valid in cuts(tokens, padded):
        k = k_ref[0, 0, start : start + size]
        v = v_ref[0, 0, start : start + size]
        w = jnp.exp2(dot_nt(k, q) * (SCALE * LOG2E) - lse)
        w = row_fill(w, valid, 0.0)
        ds = (w * (dot_nt(v, g) - delta)).astype(jnp.bfloat16)
        dv = dot_nn(w.astype(jnp.bfloat16), g)
        dk = dot_nn(ds, q) * SCALE
        dkv_ref[0, 0, start : start + valid] = dk[:valid].astype(jnp.bfloat16)
        dkv_ref[1, 0, start : start + valid] = dv[:valid].astype(jnp.bfloat16)
        part = dot_tn(k, ds)
        grad_q = part if grad_q is None else grad_q + part
    for i in range(groups):
        span = slice(i * HEAD_SIZE, (i + 1) * HEAD_SIZE)
        mix = (o_ref[0, :, span] * weight_ref[0, i : i + 1]).T
        dq = (grad_q[:, span] * SCALE).T
        if not first:
            mix = mix + mix_in_ref[:, span].astype(jnp.float32)
            dq = dq + dq_in_ref[:, span].astype(jnp.float32)
        mix_ref[:, span] = mix.astype(jnp.bfloat16)
        dq_ref[:, span] = dq.astype(jnp.bfloat16)


def forward_call(at, rows, image_kv, tokens, groups, heads):
    text = rows.shape[1]
    width = groups * HEAD_SIZE
    padded = image_kv.shape[2]
    lanes = groups * text
    stat = jax.ShapeDtypeStruct((heads, groups, text), jnp.float32)
    return pl.pallas_call(
        functools.partial(forward_kernel, tokens, groups),
        grid_spec=pltpu.PrefetchScalarGridSpec(
            num_scalar_prefetch=1,
            grid=(heads,),
            in_specs=[
                pl.BlockSpec((1, text, width), lambda h, at: (at[1], 0, h)),
                pl.BlockSpec((1, text, width), lambda h, at: (at[1], 0, heads + h)),
                pl.BlockSpec((1, 1, padded, HEAD_SIZE), lambda h, at: (0, 0, 0, at[0] * heads + h)),
                pl.BlockSpec((1, 1, padded, HEAD_SIZE), lambda h, at: (1, 0, 0, at[0] * heads + h)),
            ],
            out_specs=[
                pl.BlockSpec((1, HEAD_SIZE, lanes), lambda h, at: (h, 0, 0)),
                pl.BlockSpec((1, groups, text), lambda h, at: (h, 0, 0)),
                pl.BlockSpec((1, groups, text), lambda h, at: (h, 0, 0)),
            ],
            scratch_shapes=[pltpu.VMEM((padded, lanes), jnp.float32)],
        ),
        out_shape=[jax.ShapeDtypeStruct((heads, HEAD_SIZE, lanes), jnp.float32), stat, stat],
        compiler_params=pltpu.CompilerParams(vmem_limit_bytes=48 * 1024 * 1024),
        cost_estimate=pl.CostEstimate(
            flops=heads * 8 * padded * lanes * HEAD_SIZE,
            bytes_accessed=heads * padded * HEAD_SIZE * 4,
            transcendentals=heads * padded * lanes,
        ),
        name="forward_group",
    )(at, rows, rows, image_kv, image_kv)


def backward_call(at, rows, image_kv, mixed, lse, delta, weight, carried, grads, tokens, groups, heads):
    text = rows.shape[1]
    width = groups * HEAD_SIZE
    padded = image_kv.shape[2]
    lanes = groups * text
    first = carried is None
    stat = pl.BlockSpec((1, groups, text), lambda h, at: (h, 0, 0))
    part = pl.BlockSpec((text, width), lambda h, at: (0, h))
    in_specs = [
        pl.BlockSpec((1, text, width), lambda h, at: (at[1], 0, h)),
        pl.BlockSpec((1, text, width), lambda h, at: (at[1], 0, heads + h)),
        pl.BlockSpec((1, 1, padded, HEAD_SIZE), lambda h, at: (0, 0, 0, at[0] * heads + h)),
        pl.BlockSpec((1, 1, padded, HEAD_SIZE), lambda h, at: (1, 0, 0, at[0] * heads + h)),
        pl.BlockSpec((1, HEAD_SIZE, lanes), lambda h, at: (h, 0, 0)),
        stat,
        stat,
        stat,
    ]
    operands = [at, rows, rows, image_kv, image_kv, mixed, lse, delta, weight]
    if not first:
        in_specs += [part, pl.BlockSpec((text, width), lambda h, at: (0, heads + h))]
        operands += [carried, carried]
    aliases = {}
    in_specs.append(pl.BlockSpec(memory_space=pl.ANY))
    operands.append(grads)
    aliases = {len(operands) - 1: 2}
    grad_shape = grads.shape
    out = jax.ShapeDtypeStruct((text, heads * width), jnp.bfloat16)
    mix, dq, grads = pl.pallas_call(
        functools.partial(backward_kernel, tokens, groups, first),
        grid_spec=pltpu.PrefetchScalarGridSpec(
            num_scalar_prefetch=1,
            grid=(heads,),
            in_specs=in_specs,
            out_specs=[
                part,
                part,
                pl.BlockSpec((2, 1, tokens, HEAD_SIZE), lambda h, at: (0, 0, 0, at[0] * heads + h)),
            ],
        ),
        out_shape=[out, out, jax.ShapeDtypeStruct(grad_shape, jnp.bfloat16)],
        input_output_aliases=aliases,
        compiler_params=pltpu.CompilerParams(vmem_limit_bytes=48 * 1024 * 1024),
        cost_estimate=pl.CostEstimate(
            flops=heads * 20 * padded * lanes * HEAD_SIZE,
            bytes_accessed=heads * padded * HEAD_SIZE * 8,
            transcendentals=heads * padded * lanes,
        ),
        name="backward_group",
    )(*operands)
    return jnp.concatenate([mix, dq], axis=1), grads


def joined(first_lse, first_delta, second_lse, second_delta):
    top = jnp.maximum(first_lse, second_lse)
    first = jnp.exp2(first_lse - top)
    second = jnp.exp2(second_lse - top)
    total = first + second
    return top + jnp.log2(total), (first * first_delta + second * second_delta) / total


def shards(queries, image_key_value, image_spans, tile_counts, cross_gate, grad_out):
    seq_index = lax.axis_index("seq")
    enc_index = lax.axis_index("enc")
    enc_total = lax.axis_size("enc")
    text = queries.shape[0]
    tokens = image_key_value.shape[2]
    heads = image_key_value.shape[3] // (enc_total * HEAD_SIZE)
    groups = queries.shape[1] // (heads * HEAD_SIZE)
    row_images = enc_total // TILES
    gate = jnp.tanh(cross_gate[0])
    grad_mixed = (gate * grad_out.astype(jnp.float32)).astype(jnp.bfloat16)

    own = jnp.concatenate([queries, grad_mixed], axis=1)
    later = shifted(own, "seq", -1)
    spans = lax.dynamic_slice_in_dim(image_spans, seq_index * row_images, row_images, 0)
    offsets = spans[:, 0] - seq_index * text
    slots = jnp.arange(text, dtype=jnp.int32)
    in_own = slots[None, :] >= offsets[:, None]
    positions = jnp.where(in_own, seq_index * text, (seq_index + 1) * text) + slots[None, :]
    seen = (positions >= spans[:, :1]) & (positions < spans[:, 1:])
    window = jnp.where(in_own[:, :, None], own[None], later[None])

    padding = (-tokens) % ROW_PAD
    image_kv = jnp.pad(image_key_value, ((0, 0), (0, 0), (0, padding), (0, 0)))

    place = enc_index // TILES
    image = seq_index * row_images + place
    in_use = (enc_index - place * TILES) < lax.dynamic_index_in_dim(tile_counts, image, 0, False)
    my_seen = lax.dynamic_index_in_dim(seen, place, 0, False) & in_use
    my_own = lax.dynamic_index_in_dim(in_own, place, 0, False)

    rings = [window]
    for step in range(1, enc_total):
        rings.append(rotated(rings[-1], "enc", 1))
    places = []
    results = []
    for step in range(enc_total):
        source = lax.rem(enc_index - step + enc_total, enc_total)
        at = jnp.stack([source, place]).astype(jnp.int32)
        places.append(at)
        results.append(forward_call(at, rings[step], image_kv, tokens, groups, heads))

    lse_ring = jnp.stack([r[1] for r in results])
    delta_ring = jnp.stack([r[2] for r in results])
    lse_ring = jnp.where(my_seen, lse_ring, LOW)
    delta_ring = jnp.where(my_seen, delta_ring, 0.0)
    order = lax.rem(enc_index - jnp.arange(enc_total) + enc_total, enc_total)
    lse_all = jnp.take(lse_ring, order, axis=0)
    delta_all = jnp.take(delta_ring, order, axis=0)
    gathered = lax.all_gather(jnp.stack([lse_all, delta_all]), "enc")
    upper = None
    lower = None
    for tile in range(enc_total):
        mine = in_own[tile // TILES]
        lse_tile, delta_tile = gathered[tile, 0], gathered[tile, 1]
        up = (jnp.where(mine, lse_tile, LOW), delta_tile)
        down = (jnp.where(mine, LOW, lse_tile), delta_tile)
        upper = up if upper is None else joined(*upper, *up)
        lower = down if lower is None else joined(*lower, *down)
    edge = jnp.arange(lax.axis_size("seq"))
    before = shifted(jnp.stack(lower), "seq", 1)
    after = shifted(jnp.stack(upper), "seq", -1)
    before_lse = jnp.where(seq_index > 0, before[0], LOW)
    after_lse = jnp.where(seq_index < lax.axis_size("seq") - 1, after[0], LOW)
    own_total = joined(*upper, before_lse, before[1])
    next_total = joined(*lower, after_lse, after[1])
    full_lse = jnp.where(my_own, own_total[0], next_total[0])
    full_delta = jnp.where(my_own, own_total[1], next_total[1])
    weight_all = jnp.where(my_seen, jnp.exp2(lse_all - full_lse), 0.0) * gate
    full_lse = jnp.where(my_seen, full_lse, HIGH)

    grads = jnp.zeros(image_key_value.shape, jnp.bfloat16)
    carried = None
    for step in list(range(1, enc_total)) + [0]:
        source = places[step][0]
        if carried is not None:
            carried = rotated(carried, "enc", 1)
        pick = lambda a: lax.dynamic_index_in_dim(a, source, 0, False)
        accumulated = carried
        if row_images > 1 and carried is not None:
            accumulated = lax.dynamic_index_in_dim(carried, place, 0, False)
        message, grads = backward_call(
            places[step],
            rings[step],
            image_kv,
            results[step][0],
            pick(full_lse),
            pick(full_delta),
            pick(weight_all),
            accumulated,
            grads,
            tokens,
            groups,
            heads,
        )
        if row_images > 1:
            base = jnp.zeros((row_images,) + message.shape, message.dtype) if carried is None else carried
            message = lax.dynamic_update_index_in_dim(base, message, place, 0)
        carried = message

    sums = carried.reshape(row_images, text, -1).astype(jnp.float32)
    kept = jnp.sum(jnp.where(in_own[:, :, None], sums, 0.0), axis=0)
    passed = jnp.sum(jnp.where(in_own[:, :, None], 0.0, sums), axis=0).astype(jnp.bfloat16)
    total = (kept + shifted(passed, "seq", 1).astype(jnp.float32)).astype(jnp.bfloat16)
    width = queries.shape[1]
    return (total[:, :width], total[:, width:], grads)


def solution(mesh):
    in_specs = (
        P("seq", "enc"),
        P(None, ("seq", "enc"), None, None),
        P(),
        P(),
        P(),
        P("seq", "enc"),
    )
    out_specs = (P("seq", "enc"), P("seq", "enc"), P(None, ("seq", "enc"), None, None))
    return jax.shard_map(shards, mesh=mesh, in_specs=in_specs, out_specs=out_specs, check_vma=False)
```

```python
import functools

import jax
import jax.numpy as jnp
from jax import lax
from jax.experimental import pallas as pl
from jax.experimental.pallas import tpu as pltpu
from jax.sharding import PartitionSpec as P

HEAD_SIZE = 128
TILES = 4
LOW = -1e30
HIGH = 1e30
SCALE = HEAD_SIZE ** (-0.5)
LOG2E = 1.4426950408889634
BLOCK = 512
PAIR_ROWS = 256


def rotated(x, axis, by):
    total = lax.axis_size(axis)
    return lax.ppermute(x, axis, [(i, (i + by) % total) for i in range(total)])


def shifted(x, axis, by):
    total = lax.axis_size(axis)
    return lax.ppermute(x, axis, [(i, i + by) for i in range(total) if 0 <= i + by < total])


def dot_nt(a, b):
    return lax.dot_general(a, b, (((1,), (1,)), ((), ())), preferred_element_type=jnp.float32)


def dot_tn(a, b):
    return lax.dot_general(a, b, (((0,), (0,)), ((), ())), preferred_element_type=jnp.float32)


def dot_nn(a, b):
    return lax.dot_general(a, b, (((1,), (0,)), ((), ())), preferred_element_type=jnp.float32)


def stacked(ref, groups):
    return jnp.concatenate(
        [ref[0, :, i * HEAD_SIZE : (i + 1) * HEAD_SIZE] for i in range(groups)], axis=0
    )


def lanes_of(ref, groups):
    return jnp.concatenate([ref[0, i : i + 1] for i in range(groups)], axis=1)


def cuts(tokens):
    return [(start, min(BLOCK, tokens - start)) for start in range(0, tokens, BLOCK)]


def params():
    return pltpu.CompilerParams(vmem_limit_bytes=48 * 1024 * 1024)


def join_kernel(x_ref, o_ref):
    o_ref[:, 0, :] = x_ref[0]
    o_ref[:, 1, :] = x_ref[1]


def join_pairs(halves):
    _, tokens, width = halves.shape
    return pl.pallas_call(
        join_kernel,
        grid=(pl.cdiv(tokens, PAIR_ROWS),),
        in_specs=[pl.BlockSpec((2, PAIR_ROWS, width), lambda i: (0, i, 0))],
        out_specs=pl.BlockSpec((PAIR_ROWS, 2, width), lambda i: (i, 0, 0)),
        out_shape=jax.ShapeDtypeStruct((tokens, 2, width), halves.dtype),
        compiler_params=params(),
        cost_estimate=pl.CostEstimate(
            flops=0, bytes_accessed=4 * tokens * width * 4, transcendentals=0
        ),
        name="join_pairs",
    )(halves)


def forward_kernel(groups, at_ref, q_ref, k_ref, v_ref, o_ref, wide_ref, lse_ref, s_ref):
    parts = cuts(k_ref.shape[1])
    q = stacked(q_ref, groups)
    top = None
    for start, size in parts:
        s = dot_nt(k_ref[0, start : start + size], q)
        s_ref[start : start + size] = s
        peak = jnp.max(s, axis=0, keepdims=True)
        top = peak if top is None else jnp.maximum(top, peak)
    top = top * (SCALE * LOG2E)
    total = None
    out = None
    for start, size in parts:
        p = jnp.exp2(s_ref[start : start + size] * (SCALE * LOG2E) - top)
        part_total = jnp.sum(p, axis=0, keepdims=True)
        part_out = dot_tn(v_ref[0, start : start + size], p.astype(jnp.bfloat16))
        total = part_total if total is None else total + part_total
        out = part_out if out is None else out + part_out
    out = out / total
    lse = top + jnp.log2(total)
    wide_ref[0] = out
    for i in range(groups):
        span = slice(i * HEAD_SIZE, (i + 1) * HEAD_SIZE)
        o_ref[:, span] = out[:, span].T.astype(jnp.bfloat16)
        lse_ref[0, i : i + 1] = lse[:, span]


def delta_kernel(groups, at_ref, g_ref, wide_ref, delta_ref):
    for i in range(groups):
        span = slice(i * HEAD_SIZE, (i + 1) * HEAD_SIZE)
        g_t = g_ref[0, :, span].astype(jnp.float32).T
        delta_ref[0, i : i + 1] = jnp.sum(g_t * wide_ref[0, :, span], axis=0, keepdims=True)


def backward_kernel(groups, at_ref, q_ref, g_ref, k_ref, v_ref, lse_ref, delta_ref, *rest):
    dq_ref, dkv_ref = rest[-2:]
    q = stacked(q_ref, groups)
    g = stacked(g_ref, groups)
    lse = lanes_of(lse_ref, groups)
    delta = lanes_of(delta_ref, groups)
    grad_q = None
    for start, size in cuts(k_ref.shape[1]):
        k = k_ref[0, start : start + size]
        v = v_ref[0, start : start + size]
        w = jnp.exp2(dot_nt(k, q) * (SCALE * LOG2E) - lse)
        ds = (w * (dot_nt(v, g) - delta)).astype(jnp.bfloat16)
        dkv_ref[0, start : start + size] = (dot_nn(ds, q) * SCALE).astype(jnp.bfloat16)
        dkv_ref[1, start : start + size] = dot_nn(w.astype(jnp.bfloat16), g).astype(jnp.bfloat16)
        part = dot_tn(k, ds)
        grad_q = part if grad_q is None else grad_q + part
    for i in range(groups):
        span = slice(i * HEAD_SIZE, (i + 1) * HEAD_SIZE)
        dq_ref[:, span] = (grad_q[:, span] * SCALE).T


def row_spec(rows, groups):
    return pl.BlockSpec((1, rows.shape[1], groups * HEAD_SIZE), lambda h, at: (at[1], 0, h))


def image_specs(image_kv, heads):
    tokens = image_kv.shape[1]
    return [
        pl.BlockSpec((1, tokens, HEAD_SIZE), lambda h, at: (0, 0, at[0] * heads + h)),
        pl.BlockSpec((1, tokens, HEAD_SIZE), lambda h, at: (1, 0, at[0] * heads + h)),
    ]


def stat_spec(groups, text):
    return pl.BlockSpec((1, groups, text), lambda h, *at: (h, 0, 0))


def forward_call(at, q, image_kv, groups, heads):
    text = q.shape[1]
    width = groups * HEAD_SIZE
    tokens = image_kv.shape[1]
    lanes = groups * text
    return pl.pallas_call(
        functools.partial(forward_kernel, groups),
        grid_spec=pltpu.PrefetchScalarGridSpec(
            num_scalar_prefetch=1,
            grid=(heads,),
            in_specs=[row_spec(q, groups)] + image_specs(image_kv, heads),
            out_specs=[
                pl.BlockSpec((text, width), lambda h, at: (0, h)),
                pl.BlockSpec((1, HEAD_SIZE, lanes), lambda h, at: (h, 0, 0)),
                stat_spec(groups, text),
            ],
            scratch_shapes=[pltpu.VMEM((tokens + (-tokens) % 8, lanes), jnp.float32)],
        ),
        out_shape=[
            jax.ShapeDtypeStruct((text, heads * width), jnp.bfloat16),
            jax.ShapeDtypeStruct((heads, HEAD_SIZE, lanes), jnp.float32),
            jax.ShapeDtypeStruct((heads, groups, text), jnp.float32),
        ],
        compiler_params=params(),
        cost_estimate=pl.CostEstimate(
            flops=heads * 8 * tokens * lanes * HEAD_SIZE,
            bytes_accessed=heads * tokens * HEAD_SIZE * 4,
            transcendentals=heads * tokens * lanes,
        ),
        name="forward_group",
    )(at, q, image_kv, image_kv)


def delta_call(at, g, wide, groups, heads):
    text = g.shape[1]
    lanes = groups * text
    return pl.pallas_call(
        functools.partial(delta_kernel, groups),
        grid_spec=pltpu.PrefetchScalarGridSpec(
            num_scalar_prefetch=1,
            grid=(heads,),
            in_specs=[row_spec(g, groups), pl.BlockSpec((1, HEAD_SIZE, lanes), lambda h, at: (h, 0, 0))],
            out_specs=stat_spec(groups, text),
        ),
        out_shape=jax.ShapeDtypeStruct((heads, groups, text), jnp.float32),
        compiler_params=params(),
        cost_estimate=pl.CostEstimate(
            flops=heads * 2 * lanes * HEAD_SIZE, bytes_accessed=heads * lanes * HEAD_SIZE * 6, transcendentals=0
        ),
        name="delta_group",
    )(at, g, wide)


def backward_call(at, q, g, image_kv, lse, delta, grads, groups, heads):
    text = q.shape[1]
    width = groups * HEAD_SIZE
    tokens = image_kv.shape[1]
    lanes = groups * text
    stat = stat_spec(groups, text)
    in_specs = [row_spec(q, groups), row_spec(g, groups)] + image_specs(image_kv, heads) + [stat, stat]
    operands = [at, q, g, image_kv, image_kv, lse, delta]
    aliases = {}
    if grads is not None:
        in_specs.append(pl.BlockSpec(memory_space=pl.ANY))
        aliases = {len(operands): 1}
        operands.append(grads)
    return pl.pallas_call(
        functools.partial(backward_kernel, groups),
        grid_spec=pltpu.PrefetchScalarGridSpec(
            num_scalar_prefetch=1,
            grid=(heads,),
            in_specs=in_specs,
            out_specs=[
                pl.BlockSpec((text, width), lambda h, at: (0, h)),
                pl.BlockSpec((2, tokens, HEAD_SIZE), lambda h, at: (0, 0, at[0] * heads + h)),
            ],
        ),
        out_shape=[
            jax.ShapeDtypeStruct((text, heads * width), jnp.float32),
            jax.ShapeDtypeStruct(image_kv.shape, jnp.bfloat16),
        ],
        input_output_aliases=aliases,
        compiler_params=params(),
        cost_estimate=pl.CostEstimate(
            flops=heads * 20 * tokens * lanes * HEAD_SIZE,
            bytes_accessed=heads * tokens * HEAD_SIZE * 8,
            transcendentals=heads * tokens * lanes,
        ),
        name="backward_group",
    )(*operands)


def mix_kernel(groups, o_ref, own_ref, old_ref, carried_ref, out_ref):
    own = own_ref[0].T
    old = old_ref[0].T
    for i in range(groups):
        span = slice(i * HEAD_SIZE, (i + 1) * HEAD_SIZE)
        mix = o_ref[:, span].astype(jnp.float32) * own[:, i : i + 1]
        mix = mix + carried_ref[:, span].astype(jnp.float32) * old[:, i : i + 1]
        out_ref[:, span] = mix.astype(jnp.bfloat16)


def mix_call(out, own, old, carried):
    heads, groups, text = own.shape
    width = groups * HEAD_SIZE
    rows = pl.BlockSpec((text, width), lambda h: (0, h))
    return pl.pallas_call(
        functools.partial(mix_kernel, groups),
        grid=(heads,),
        in_specs=[rows, stat_spec(groups, text), stat_spec(groups, text), rows],
        out_specs=rows,
        out_shape=jax.ShapeDtypeStruct((text, heads * width), jnp.bfloat16),
        compiler_params=params(),
        cost_estimate=pl.CostEstimate(
            flops=4 * text * heads * width, bytes_accessed=6 * text * heads * width, transcendentals=0
        ),
        name="mix_group",
    )(out, own, old, carried)


def merged(lse, delta):
    top = jnp.max(lse, axis=0)
    share = jnp.exp2(lse - top)
    total = jnp.sum(share, axis=0)
    return top + jnp.log2(total), jnp.sum(share * delta, axis=0) / total


def shards(queries, image_key_value, image_spans, tile_counts, cross_gate, grad_out):
    seq_index = lax.axis_index("seq")
    seq_total = lax.axis_size("seq")
    enc_index = lax.axis_index("enc")
    enc_total = lax.axis_size("enc")
    text, width = queries.shape
    heads = image_key_value.shape[3] // (enc_total * HEAD_SIZE)
    groups = width // (heads * HEAD_SIZE)
    row_images = enc_total // TILES
    gate = jnp.tanh(cross_gate[0])
    steps = range(enc_total)

    spans = lax.dynamic_slice_in_dim(image_spans, seq_index * row_images, row_images, 0)
    offsets = spans[:, 0] - seq_index * text
    slots = jnp.arange(text, dtype=jnp.int32)
    in_own = slots[None, :] >= offsets[:, None]
    positions = jnp.where(in_own, seq_index * text, (seq_index + 1) * text) + slots[None, :]
    seen = (positions >= spans[:, :1]) & (positions < spans[:, 1:])

    sources = [lax.rem(enc_index - step + enc_total, enc_total) for step in steps]
    places = [source // TILES for source in sources]
    ats = [jnp.stack([source, places[0]]).astype(jnp.int32) for source in sources]
    counts = lax.dynamic_slice_in_dim(tile_counts, seq_index * row_images, row_images, 0)

    def of_place(x):
        return x[0] if row_images == 1 else lax.dynamic_index_in_dim(x, places[0], 0, False)

    def of_group(x, step):
        return lax.dynamic_index_in_dim(x, sources[step], 0, False)

    def placed(message, carried):
        if row_images == 1:
            return message
        base = jnp.zeros((row_images,) + message.shape, message.dtype) if carried is None else carried
        return lax.dynamic_update_index_in_dim(base, message, places[0], 0)

    in_use = (enc_index - places[0] * TILES) < of_place(counts)
    my_seen = of_place(seen) & in_use
    wide_own = in_own[:, None, None, None, :]
    order = jnp.stack(sources)

    def window(own, later):
        return jnp.where(in_own[:, :, None], own[None], later[None])

    grad_mixed = (gate * grad_out.astype(jnp.float32)).astype(jnp.bfloat16)
    q_moving = window(queries, shifted(queries, "seq", -1))
    q_first, g_later = lax.optimization_barrier((q_moving, shifted(grad_mixed, "seq", -1)))
    q_rings = [q_first]
    g_rings = [window(grad_mixed, g_later)]
    image_kv = image_key_value[:, 0]
    outs, wides, lse_ring, delta_ring = [], [], [], []
    for step in steps:
        more = step + 1 < enc_total
        if more:
            q_next = rotated(q_moving if step == 0 else q_rings[step], "enc", 1)
            if step == 0:
                q_next, image_kv = lax.optimization_barrier((q_next, image_kv))
            q_rings.append(q_next)
        out, wide, lse = forward_call(ats[step], q_rings[step], image_kv, groups, heads)
        outs.append(out)
        wides.append(wide)
        if step > 0:
            g_next, lse = lax.optimization_barrier((g_next, lse))
            g_rings.append(g_next)
        lse_ring.append(lse)
        if more:
            g_next = rotated(g_rings[step], "enc", 1)
        delta_ring.append(delta_call(ats[step], g_rings[step], wides[step], groups, heads))

    lse_mine = jnp.take(jnp.where(my_seen, jnp.stack(lse_ring), LOW), order, axis=0)
    delta_mine = jnp.take(jnp.stack(delta_ring), order, axis=0)
    mine = jnp.stack([lse_mine, delta_mine])
    early = row_images == 1
    tiles = [mine] + [rotated(mine, "enc", step) for step in steps[1:]]
    tile_lse = jnp.stack([t[0] for t in tiles])
    tile_delta = jnp.stack([t[1] for t in tiles])
    if early:
        first_out, tile_lse = lax.optimization_barrier((outs[1], tile_lse))
        mix_carried = rotated(first_out, "enc", 1)
    image_lse, image_delta = [], []
    for a in range(row_images):
        lse_a = tile_lse
        if row_images > 1:
            lse_a = jnp.where((jnp.stack(places) == a)[:, None, None, None, None], lse_a, LOW)
        lse_a, delta_a = merged(lse_a, tile_delta)
        image_lse.append(lse_a)
        image_delta.append(delta_a)
    image_lse, image_delta = jnp.stack(image_lse), jnp.stack(image_delta)
    upper = merged(jnp.where(wide_own, image_lse, LOW), image_delta)
    lower = merged(jnp.where(wide_own, LOW, image_lse), image_delta)
    lower, upper = lax.optimization_barrier((jnp.stack(lower), jnp.stack(upper)))
    from_before = shifted(lower, "seq", 1)
    from_after = shifted(upper, "seq", -1)
    if early:
        from_before, from_after, mix_carried = lax.optimization_barrier((from_before, from_after, mix_carried))
    before_lse = jnp.where(seq_index > 0, from_before[0], LOW)
    after_lse = jnp.where(seq_index < seq_total - 1, from_after[0], LOW)
    own_total = merged(jnp.stack([upper[0], before_lse]), jnp.stack([upper[1], from_before[1]]))
    next_total = merged(jnp.stack([lower[0], after_lse]), jnp.stack([lower[1], from_after[1]]))
    full_lse = jnp.where(wide_own, own_total[0], next_total[0])
    full_delta = jnp.where(wide_own, own_total[1], next_total[1])
    mine_share = jnp.where(my_seen, jnp.exp2(lse_mine - of_place(image_lse)), 0.0)
    home_share = jnp.where(full_lse > LOW / 2, jnp.exp2(image_lse - full_lse), 0.0) * gate
    lse_used = jnp.where(my_seen, of_place(full_lse), HIGH)
    delta_used = of_place(full_delta)

    def mixed(step, carried):
        share = of_group(mine_share, step)
        if carried is None:
            return mix_call(outs[step], share, share, jnp.zeros((text, width), jnp.bfloat16))
        old = jnp.ones_like(share)
        if early and step == 2:
            old = jnp.exp2(of_group(tile_lse[1], step) - of_group(of_place(image_lse), step))
        if early and step == 0:
            home = of_group(home_share[0], 0)
            share, old = share * home, old * home
        return mix_call(outs[step], share, old, of_place(carried) if row_images > 1 else carried)

    def homing(sums):
        sums = sums.reshape(row_images, text, width).astype(jnp.float32)
        kept = jnp.sum(jnp.where(in_own[:, :, None], sums, 0.0), axis=0)
        passed = jnp.sum(jnp.where(in_own[:, :, None], 0.0, sums), axis=0).astype(jnp.bfloat16)
        return kept, shifted(passed, "seq", 1)

    def homed(kept, passed):
        return (kept + passed.astype(jnp.float32)).astype(jnp.bfloat16)

    def scaled_home(sums):
        if early:
            return sums
        shares = jnp.stack([of_group(home_share[a], 0) for a in range(row_images)])
        shares = shares.reshape(row_images, heads * groups, text).transpose(0, 2, 1)
        parts = sums.reshape(row_images, text, heads * groups, HEAD_SIZE).astype(jnp.float32)
        return (parts * shares[..., None]).reshape(row_images, text, width).astype(jnp.bfloat16)

    if not early:
        mix_carried = rotated(placed(mixed(1, None), None), "enc", 1)
    mix_carried = placed(mixed(2, mix_carried), mix_carried)
    mix_moving = rotated(mix_carried, "enc", 1)
    grads = None
    carried = None
    for step in list(steps[1:]) + [0]:
        q = q_rings[step]
        grad_q, grads = backward_call(
            ats[step], q, g_rings[step], image_kv, of_group(lse_used, step), of_group(delta_used, step),
            grads, groups, heads,
        )
        if step == 0:
            grad_q, mix_passed = lax.optimization_barrier((grad_q, mix_passed))
        if carried is not None:
            grad_q = grad_q + (carried if row_images == 1 else of_place(carried)).astype(jnp.float32)
        carried = placed(grad_q.astype(jnp.bfloat16), carried)
        if step > 0:
            carried = rotated(carried, "enc", 1)
        following = 0 if step + 2 > enc_total else step + 2
        if 0 < step and (step + 2) <= enc_total:
            mix_moving, grads = lax.optimization_barrier((mix_moving, grads))
            mix_carried = placed(mixed(following % enc_total, mix_moving), mix_moving)
            if following % enc_total:
                mix_moving = rotated(mix_carried, "enc", 1)
            else:
                mix_kept, mix_passed = homing(scaled_home(mix_carried))
    grads = join_pairs(grads).transpose(1, 0, 2).reshape(image_key_value.shape)

    grad_kept, grad_passed = homing(carried)
    return (homed(mix_kept, mix_passed), homed(grad_kept, grad_passed), grads)


def solution(mesh):
    in_specs = (
        P("seq", "enc"),
        P(None, ("seq", "enc"), None, None),
        P(),
        P(),
        P(),
        P("seq", "enc"),
    )
    out_specs = (P("seq", "enc"), P("seq", "enc"), P(None, ("seq", "enc"), None, None))
    return jax.shard_map(shards, mesh=mesh, in_specs=in_specs, out_specs=out_specs, check_vma=False)
```

```python
import functools

import jax
import jax.numpy as jnp
from jax import lax
from jax.experimental import pallas as pl
from jax.experimental.pallas import tpu as pltpu
from jax.sharding import PartitionSpec as P

HEAD_SIZE = 128
TILES = 4
LOW = -1e30
HIGH = 1e30
SCALE = HEAD_SIZE ** (-0.5)
LOG2E = 1.4426950408889634
BLOCK = 512
PAIR_ROWS = 256
TOGETHER = 2


def rotated(x, axis, by):
    total = lax.axis_size(axis)
    return lax.ppermute(x, axis, [(i, (i + by) % total) for i in range(total)])


def shifted(x, axis, by):
    total = lax.axis_size(axis)
    return lax.ppermute(x, axis, [(i, i + by) for i in range(total) if 0 <= i + by < total])


def dot_nt(a, b):
    return lax.dot_general(a, b, (((1,), (1,)), ((), ())), preferred_element_type=jnp.float32)


def dot_tn(a, b):
    return lax.dot_general(a, b, (((0,), (0,)), ((), ())), preferred_element_type=jnp.float32)


def dot_nn(a, b):
    return lax.dot_general(a, b, (((1,), (0,)), ((), ())), preferred_element_type=jnp.float32)


def stacked(ref, groups):
    return jnp.concatenate(
        [ref[0, :, i * HEAD_SIZE : (i + 1) * HEAD_SIZE] for i in range(groups)], axis=0
    )


def cuts(tokens):
    return [(start, min(BLOCK, tokens - start)) for start in range(0, tokens, BLOCK)]


def params():
    return pltpu.CompilerParams(vmem_limit_bytes=44 * 1024 * 1024)


def join_kernel(x_ref, o_ref):
    o_ref[:, 0, :] = x_ref[0]
    o_ref[:, 1, :] = x_ref[1]


def join_pairs(halves):
    _, tokens, width = halves.shape
    return pl.pallas_call(
        join_kernel,
        grid=(pl.cdiv(tokens, PAIR_ROWS),),
        in_specs=[pl.BlockSpec((2, PAIR_ROWS, width), lambda i: (0, i, 0))],
        out_specs=pl.BlockSpec((PAIR_ROWS, 2, width), lambda i: (i, 0, 0)),
        out_shape=jax.ShapeDtypeStruct((tokens, 2, width), halves.dtype),
        compiler_params=params(),
        cost_estimate=pl.CostEstimate(
            flops=0, bytes_accessed=4 * tokens * width * 4, transcendentals=0
        ),
        name="join_pairs",
    )(halves)


def forward_kernel(groups, at_ref, q_ref, k_ref, v_ref, o_ref, wide_ref, lse_ref, s_ref):
    parts = cuts(k_ref.shape[1])
    q = stacked(q_ref, groups)
    top = None
    for start, size in parts:
        s = dot_nt(k_ref[0, start : start + size], q)
        s_ref[start : start + size] = s
        peak = jnp.max(s, axis=0, keepdims=True)
        top = peak if top is None else jnp.maximum(top, peak)
    top = top * (SCALE * LOG2E)
    total = None
    out = None
    for start, size in parts:
        p = jnp.exp2(s_ref[start : start + size] * (SCALE * LOG2E) - top)
        part_total = jnp.sum(p, axis=0, keepdims=True)
        part_out = dot_tn(v_ref[0, start : start + size], p.astype(jnp.bfloat16))
        total = part_total if total is None else total + part_total
        out = part_out if out is None else out + part_out
    out = out / total
    lse = top + jnp.log2(total)
    wide_ref[0] = out
    for i in range(groups):
        span = slice(i * HEAD_SIZE, (i + 1) * HEAD_SIZE)
        o_ref[:, span] = out[:, span].T.astype(jnp.bfloat16)
        lse_ref[0, i : i + 1] = lse[:, span]


def delta_kernel(groups, at_ref, g_ref, wide_ref, delta_ref):
    for i in range(groups):
        span = slice(i * HEAD_SIZE, (i + 1) * HEAD_SIZE)
        g_t = g_ref[0, :, span].astype(jnp.float32).T
        delta_ref[0, i : i + 1] = jnp.sum(g_t * wide_ref[0, :, span], axis=0, keepdims=True)


def backward_kernel(groups, at_ref, q_ref, g_ref, k_ref, v_ref, lse_ref, delta_ref, *rest):
    dq_ref, dkv_ref = rest[-2:]
    k = k_ref[0]
    v = v_ref[0]
    lse_columns = lse_ref[0].T
    delta_columns = delta_ref[0].T
    dk = dv = None
    for first in range(0, groups, TOGETHER):
        members = range(first, first + TOGETHER)

        def rows(ref):
            return jnp.concatenate([ref[0, :, i * HEAD_SIZE : (i + 1) * HEAD_SIZE] for i in members], axis=0)

        def column(values):
            return jnp.concatenate([values[:, i : i + 1] for i in members], axis=0)

        q = rows(q_ref)
        g = rows(g_ref)
        w = jnp.exp2(dot_nt(q, k) * (SCALE * LOG2E) - column(lse_columns))
        ds = (w * (dot_nt(g, v) - column(delta_columns))).astype(jnp.bfloat16)
        dq = dot_nn(ds, k) * SCALE
        part_k = dot_tn(q, ds)
        part_v = dot_tn(g, w.astype(jnp.bfloat16))
        dk = part_k if dk is None else dk + part_k
        dv = part_v if dv is None else dv + part_v
        for i in members:
            start = (i - first) * dq_ref.shape[0]
            dq_ref[:, i * HEAD_SIZE : (i + 1) * HEAD_SIZE] = dq[start : start + dq_ref.shape[0]]
    dkv_ref[0] = (dk * SCALE).T.astype(jnp.bfloat16)
    dkv_ref[1] = dv.T.astype(jnp.bfloat16)


def row_spec(rows, groups):
    return pl.BlockSpec((1, rows.shape[1], groups * HEAD_SIZE), lambda h, at: (at[1], 0, h))


def image_specs(image_kv, heads):
    tokens = image_kv.shape[1]
    return [
        pl.BlockSpec((1, tokens, HEAD_SIZE), lambda h, at: (0, 0, at[0] * heads + h)),
        pl.BlockSpec((1, tokens, HEAD_SIZE), lambda h, at: (1, 0, at[0] * heads + h)),
    ]


def stat_spec(groups, text):
    return pl.BlockSpec((1, groups, text), lambda h, *at: (h, 0, 0))


def forward_call(at, q, image_kv, groups, heads):
    text = q.shape[1]
    width = groups * HEAD_SIZE
    tokens = image_kv.shape[1]
    lanes = groups * text
    return pl.pallas_call(
        functools.partial(forward_kernel, groups),
        grid_spec=pltpu.PrefetchScalarGridSpec(
            num_scalar_prefetch=1,
            grid=(heads,),
            in_specs=[row_spec(q, groups)] + image_specs(image_kv, heads),
            out_specs=[
                pl.BlockSpec((text, width), lambda h, at: (0, h)),
                pl.BlockSpec((1, HEAD_SIZE, lanes), lambda h, at: (h, 0, 0)),
                stat_spec(groups, text),
            ],
            scratch_shapes=[pltpu.VMEM((tokens + (-tokens) % 8, lanes), jnp.float32)],
        ),
        out_shape=[
            jax.ShapeDtypeStruct((text, heads * width), jnp.bfloat16),
            jax.ShapeDtypeStruct((heads, HEAD_SIZE, lanes), jnp.float32),
            jax.ShapeDtypeStruct((heads, groups, text), jnp.float32),
        ],
        compiler_params=params(),
        cost_estimate=pl.CostEstimate(
            flops=heads * 8 * tokens * lanes * HEAD_SIZE,
            bytes_accessed=heads * tokens * HEAD_SIZE * 4,
            transcendentals=heads * tokens * lanes,
        ),
        name="forward_group",
    )(at, q, image_kv, image_kv)


def delta_call(at, g, wide, groups, heads):
    text = g.shape[1]
    lanes = groups * text
    return pl.pallas_call(
        functools.partial(delta_kernel, groups),
        grid_spec=pltpu.PrefetchScalarGridSpec(
            num_scalar_prefetch=1,
            grid=(heads,),
            in_specs=[row_spec(g, groups), pl.BlockSpec((1, HEAD_SIZE, lanes), lambda h, at: (h, 0, 0))],
            out_specs=stat_spec(groups, text),
        ),
        out_shape=jax.ShapeDtypeStruct((heads, groups, text), jnp.float32),
        compiler_params=params(),
        cost_estimate=pl.CostEstimate(
            flops=heads * 2 * lanes * HEAD_SIZE, bytes_accessed=heads * lanes * HEAD_SIZE * 6, transcendentals=0
        ),
        name="delta_group",
    )(at, g, wide)


def backward_call(at, q, g, image_kv, lse, delta, grads, groups, heads):
    text = q.shape[1]
    width = groups * HEAD_SIZE
    tokens = image_kv.shape[1]
    lanes = groups * text
    stat = stat_spec(groups, text)
    in_specs = [row_spec(q, groups), row_spec(g, groups)] + image_specs(image_kv, heads) + [stat, stat]
    operands = [at, q, g, image_kv, image_kv, lse, delta]
    aliases = {}
    if grads is not None:
        in_specs.append(pl.BlockSpec(memory_space=pl.ANY))
        aliases = {len(operands): 1}
        operands.append(grads)
    return pl.pallas_call(
        functools.partial(backward_kernel, groups),
        grid_spec=pltpu.PrefetchScalarGridSpec(
            num_scalar_prefetch=1,
            grid=(heads,),
            in_specs=in_specs,
            out_specs=[
                pl.BlockSpec((text, width), lambda h, at: (0, h)),
                pl.BlockSpec((2, tokens, HEAD_SIZE), lambda h, at: (0, 0, at[0] * heads + h)),
            ],
        ),
        out_shape=[
            jax.ShapeDtypeStruct((text, heads * width), jnp.float32),
            jax.ShapeDtypeStruct(image_kv.shape, jnp.bfloat16),
        ],
        input_output_aliases=aliases,
        compiler_params=params(),
        cost_estimate=pl.CostEstimate(
            flops=heads * 20 * tokens * lanes * HEAD_SIZE,
            bytes_accessed=heads * tokens * HEAD_SIZE * 8,
            transcendentals=heads * tokens * lanes,
        ),
        name="backward_group",
    )(*operands)


def mix_kernel(groups, o_ref, own_ref, old_ref, carried_ref, out_ref):
    own = own_ref[0].T
    old = old_ref[0].T
    for i in range(groups):
        span = slice(i * HEAD_SIZE, (i + 1) * HEAD_SIZE)
        mix = o_ref[:, span].astype(jnp.float32) * own[:, i : i + 1]
        mix = mix + carried_ref[:, span].astype(jnp.float32) * old[:, i : i + 1]
        out_ref[:, span] = mix.astype(jnp.bfloat16)


def mix_call(out, own, old, carried):
    heads, groups, text = own.shape
    width = groups * HEAD_SIZE
    rows = pl.BlockSpec((text, width), lambda h: (0, h))
    return pl.pallas_call(
        functools.partial(mix_kernel, groups),
        grid=(heads,),
        in_specs=[rows, stat_spec(groups, text), stat_spec(groups, text), rows],
        out_specs=rows,
        out_shape=jax.ShapeDtypeStruct((text, heads * width), jnp.bfloat16),
        compiler_params=params(),
        cost_estimate=pl.CostEstimate(
            flops=4 * text * heads * width, bytes_accessed=6 * text * heads * width, transcendentals=0
        ),
        name="mix_group",
    )(out, own, old, carried)


def merged(lse, delta):
    top = jnp.max(lse, axis=0)
    share = jnp.exp2(lse - top)
    total = jnp.sum(share, axis=0)
    return top + jnp.log2(total), jnp.sum(share * delta, axis=0) / total


def shards(queries, image_key_value, image_spans, tile_counts, cross_gate, grad_out):
    seq_index = lax.axis_index("seq")
    seq_total = lax.axis_size("seq")
    enc_index = lax.axis_index("enc")
    enc_total = lax.axis_size("enc")
    text, width = queries.shape
    heads = image_key_value.shape[3] // (enc_total * HEAD_SIZE)
    groups = width // (heads * HEAD_SIZE)
    row_images = enc_total // TILES
    gate = jnp.tanh(cross_gate[0])
    steps = range(enc_total)

    spans = lax.dynamic_slice_in_dim(image_spans, seq_index * row_images, row_images, 0)
    offsets = spans[:, 0] - seq_index * text
    slots = jnp.arange(text, dtype=jnp.int32)
    in_own = slots[None, :] >= offsets[:, None]
    positions = jnp.where(in_own, seq_index * text, (seq_index + 1) * text) + slots[None, :]
    seen = (positions >= spans[:, :1]) & (positions < spans[:, 1:])

    sources = [lax.rem(enc_index - step + enc_total, enc_total) for step in steps]
    places = [source // TILES for source in sources]
    ats = [jnp.stack([source, places[0]]).astype(jnp.int32) for source in sources]
    counts = lax.dynamic_slice_in_dim(tile_counts, seq_index * row_images, row_images, 0)

    def of_place(x):
        return x[0] if row_images == 1 else lax.dynamic_index_in_dim(x, places[0], 0, False)

    def of_group(x, step):
        return lax.dynamic_index_in_dim(x, sources[step], 0, False)

    def placed(message, carried):
        if row_images == 1:
            return message
        base = jnp.zeros((row_images,) + message.shape, message.dtype) if carried is None else carried
        return lax.dynamic_update_index_in_dim(base, message, places[0], 0)

    in_use = (enc_index - places[0] * TILES) < of_place(counts)
    my_seen = of_place(seen) & in_use
    wide_own = in_own[:, None, None, None, :]
    order = jnp.stack(sources)

    def window(own, later):
        return jnp.where(in_own[:, :, None], own[None], later[None])

    q_later, grad_out = lax.optimization_barrier((shifted(queries, "seq", -1), grad_out))
    q_moving = window(queries, q_later)
    grad_mixed = (gate * grad_out.astype(jnp.float32)).astype(jnp.bfloat16)
    q_first, g_later, image_kv = lax.optimization_barrier(
        (q_moving, shifted(grad_mixed, "seq", -1), image_key_value)
    )
    q_rings = [q_first]
    g_rings = [window(grad_mixed, g_later)]
    image_kv = image_kv[:, 0]
    outs, wides, lse_ring, delta_ring = [], [], [], []
    for step in steps:
        more = step + 1 < enc_total
        if more:
            q_next = rotated(q_moving if step == 0 else q_rings[step], "enc", 1)
            if step == 0:
                q_next, image_kv = lax.optimization_barrier((q_next, image_kv))
            q_rings.append(q_next)
        out, wide, lse = forward_call(ats[step], q_rings[step], image_kv, groups, heads)
        outs.append(out)
        wides.append(wide)
        if step > 0:
            g_next, lse = lax.optimization_barrier((g_next, lse))
            g_rings.append(g_next)
        lse_ring.append(lse)
        if more:
            g_next = rotated(g_rings[step], "enc", 1)
        delta_ring.append(delta_call(ats[step], g_rings[step], wides[step], groups, heads))

    lse_mine = jnp.take(jnp.where(my_seen, jnp.stack(lse_ring), LOW), order, axis=0)
    delta_mine = jnp.take(jnp.stack(delta_ring), order, axis=0)
    mine = jnp.stack([lse_mine, delta_mine])
    early = row_images == 1
    tiles = [mine] + [rotated(mine, "enc", step) for step in steps[1:]]
    tile_lse = jnp.stack([t[0] for t in tiles])
    tile_delta = jnp.stack([t[1] for t in tiles])
    if early:
        first_out, tile_lse = lax.optimization_barrier((outs[1], tile_lse))
        mix_carried = rotated(first_out, "enc", 1)
    image_lse, image_delta = [], []
    for a in range(row_images):
        lse_a = tile_lse
        if row_images > 1:
            lse_a = jnp.where((jnp.stack(places) == a)[:, None, None, None, None], lse_a, LOW)
        lse_a, delta_a = merged(lse_a, tile_delta)
        image_lse.append(lse_a)
        image_delta.append(delta_a)
    image_lse, image_delta = jnp.stack(image_lse), jnp.stack(image_delta)
    upper = merged(jnp.where(wide_own, image_lse, LOW), image_delta)
    lower = merged(jnp.where(wide_own, LOW, image_lse), image_delta)
    lower, upper = lax.optimization_barrier((jnp.stack(lower), jnp.stack(upper)))
    from_before = shifted(lower, "seq", 1)
    from_after = shifted(upper, "seq", -1)
    if early:
        from_before, from_after, mix_carried = lax.optimization_barrier((from_before, from_after, mix_carried))
    before_lse = jnp.where(seq_index > 0, from_before[0], LOW)
    after_lse = jnp.where(seq_index < seq_total - 1, from_after[0], LOW)
    own_total = merged(jnp.stack([upper[0], before_lse]), jnp.stack([upper[1], from_before[1]]))
    next_total = merged(jnp.stack([lower[0], after_lse]), jnp.stack([lower[1], from_after[1]]))
    full_lse = jnp.where(wide_own, own_total[0], next_total[0])
    full_delta = jnp.where(wide_own, own_total[1], next_total[1])
    mine_share = jnp.where(my_seen, jnp.exp2(lse_mine - of_place(image_lse)), 0.0)
    home_share = jnp.where(full_lse > LOW / 2, jnp.exp2(image_lse - full_lse), 0.0) * gate
    lse_used = jnp.where(my_seen, of_place(full_lse), HIGH)
    delta_used = of_place(full_delta)

    def mixed(step, carried):
        share = of_group(mine_share, step)
        if carried is None:
            return mix_call(outs[step], share, share, jnp.zeros((text, width), jnp.bfloat16))
        old = jnp.ones_like(share)
        if early and step == 2:
            old = jnp.exp2(of_group(tile_lse[1], step) - of_group(of_place(image_lse), step))
        if early and step == 0:
            home = of_group(home_share[0], 0)
            share, old = share * home, old * home
        return mix_call(outs[step], share, old, of_place(carried) if row_images > 1 else carried)

    def homing(sums):
        sums = sums.reshape(row_images, text, width).astype(jnp.float32)
        kept = jnp.sum(jnp.where(in_own[:, :, None], sums, 0.0), axis=0)
        passed = jnp.sum(jnp.where(in_own[:, :, None], 0.0, sums), axis=0).astype(jnp.bfloat16)
        return kept, shifted(passed, "seq", 1)

    def homed(kept, passed):
        return (kept + passed.astype(jnp.float32)).astype(jnp.bfloat16)

    def scaled_home(sums):
        if early:
            return sums
        shares = jnp.stack([of_group(home_share[a], 0) for a in range(row_images)])
        shares = shares.reshape(row_images, heads * groups, text).transpose(0, 2, 1)
        parts = sums.reshape(row_images, text, heads * groups, HEAD_SIZE).astype(jnp.float32)
        return (parts * shares[..., None]).reshape(row_images, text, width).astype(jnp.bfloat16)

    if not early:
        mix_carried = rotated(placed(mixed(1, None), None), "enc", 1)
    mix_carried = placed(mixed(2, mix_carried), mix_carried)
    mix_moving = rotated(mix_carried, "enc", 1)
    grads = None
    carried = None
    for step in list(steps[1:]) + [0]:
        q = q_rings[step]
        grad_q, grads = backward_call(
            ats[step], q, g_rings[step], image_kv, of_group(lse_used, step), of_group(delta_used, step),
            grads, groups, heads,
        )
        if step == 0:
            grad_q, mix_passed = lax.optimization_barrier((grad_q, mix_passed))
        if carried is not None:
            grad_q = grad_q + (carried if row_images == 1 else of_place(carried)).astype(jnp.float32)
        carried = placed(grad_q.astype(jnp.bfloat16), carried)
        if step > 0:
            carried = rotated(carried, "enc", 1)
        if 0 < step < enc_total - 1:
            following = (step + 2) % enc_total
            if following == 0:
                continue
            mix_moving, grads = lax.optimization_barrier((mix_moving, grads))
            mix_carried = placed(mixed(following, mix_moving), mix_moving)
            mix_moving = rotated(mix_carried, "enc", 1)
        elif step > 0:
            mix_moving, grads = lax.optimization_barrier((mix_moving, grads))
            mix_carried = placed(mixed(0, mix_moving), mix_moving)
            mix_kept, mix_passed = homing(scaled_home(mix_carried))
    grads = join_pairs(grads).transpose(1, 0, 2).reshape(image_key_value.shape)

    grad_kept, grad_passed = homing(carried)
    return (homed(mix_kept, mix_passed), homed(grad_kept, grad_passed), grads)


def solution(mesh):
    in_specs = (
        P("seq", "enc"),
        P(None, ("seq", "enc"), None, None),
        P(),
        P(),
        P(),
        P("seq", "enc"),
    )
    out_specs = (P("seq", "enc"), P("seq", "enc"), P(None, ("seq", "enc"), None, None))
    return jax.shard_map(shards, mesh=mesh, in_specs=in_specs, out_specs=out_specs, check_vma=False)
```

```python
import functools

import jax
import jax.numpy as jnp
from jax import lax
from jax.experimental import pallas as pl
from jax.experimental.pallas import tpu as pltpu
from jax.sharding import PartitionSpec as P

HEAD_SIZE = 128
TILES = 4
LOW = -1e30
HIGH = 1e30
SCALE = HEAD_SIZE ** (-0.5)
LOG2E = 1.4426950408889634
BLOCK = 512
PAIR_ROWS = 256
TOGETHER = 2


def rotated(x, axis, by):
    total = lax.axis_size(axis)
    return lax.ppermute(x, axis, [(i, (i + by) % total) for i in range(total)])


def shifted(x, axis, by):
    total = lax.axis_size(axis)
    return lax.ppermute(x, axis, [(i, i + by) for i in range(total) if 0 <= i + by < total])


def dot_nt(a, b):
    return lax.dot_general(a, b, (((1,), (1,)), ((), ())), preferred_element_type=jnp.float32)


def dot_tn(a, b):
    return lax.dot_general(a, b, (((0,), (0,)), ((), ())), preferred_element_type=jnp.float32)


def dot_nn(a, b):
    return lax.dot_general(a, b, (((1,), (0,)), ((), ())), preferred_element_type=jnp.float32)


def stacked(ref, groups):
    return jnp.concatenate(
        [ref[0, :, i * HEAD_SIZE : (i + 1) * HEAD_SIZE] for i in range(groups)], axis=0
    )


def cuts(tokens):
    return [(start, min(BLOCK, tokens - start)) for start in range(0, tokens, BLOCK)]


def params():
    return pltpu.CompilerParams(vmem_limit_bytes=48 * 1024 * 1024)


def join_kernel(x_ref, o_ref):
    o_ref[:, 0, :] = x_ref[0]
    o_ref[:, 1, :] = x_ref[1]


def join_pairs(halves):
    _, tokens, width = halves.shape
    return pl.pallas_call(
        join_kernel,
        grid=(pl.cdiv(tokens, PAIR_ROWS),),
        in_specs=[pl.BlockSpec((2, PAIR_ROWS, width), lambda i: (0, i, 0))],
        out_specs=pl.BlockSpec((PAIR_ROWS, 2, width), lambda i: (i, 0, 0)),
        out_shape=jax.ShapeDtypeStruct((tokens, 2, width), halves.dtype),
        compiler_params=pltpu.CompilerParams(vmem_limit_bytes=16 * 1024 * 1024),
        cost_estimate=pl.CostEstimate(
            flops=0, bytes_accessed=4 * tokens * width * 4, transcendentals=0
        ),
        name="join_pairs",
    )(halves)


def forward_kernel(groups, at_ref, q_ref, k_ref, v_ref, o_ref, wide_ref, lse_ref, s_ref):
    parts = cuts(k_ref.shape[1])
    q = stacked(q_ref, groups)
    top = None
    for start, size in parts:
        s = dot_nt(k_ref[0, start : start + size], q)
        s_ref[start : start + size] = s
        peak = jnp.max(s, axis=0, keepdims=True)
        top = peak if top is None else jnp.maximum(top, peak)
    top = top * (SCALE * LOG2E)
    total = None
    out = None
    for start, size in parts:
        p = jnp.exp2(s_ref[start : start + size] * (SCALE * LOG2E) - top)
        part_total = jnp.sum(p, axis=0, keepdims=True)
        part_out = dot_tn(v_ref[0, start : start + size], p.astype(jnp.bfloat16))
        total = part_total if total is None else total + part_total
        out = part_out if out is None else out + part_out
    out = out / total
    lse = top + jnp.log2(total)
    wide_ref[0] = out
    for i in range(groups):
        span = slice(i * HEAD_SIZE, (i + 1) * HEAD_SIZE)
        o_ref[:, span] = out[:, span].T.astype(jnp.bfloat16)
        lse_ref[0, i : i + 1] = lse[:, span]


def delta_kernel(groups, at_ref, g_ref, wide_ref, delta_ref):
    for i in range(groups):
        span = slice(i * HEAD_SIZE, (i + 1) * HEAD_SIZE)
        g_t = g_ref[0, :, span].astype(jnp.float32).T
        delta_ref[0, i : i + 1] = jnp.sum(g_t * wide_ref[0, :, span], axis=0, keepdims=True)


def backward_kernel(groups, at_ref, q_ref, g_ref, k_ref, v_ref, lse_ref, delta_ref, *rest):
    dq_ref, dkv_ref = rest[-2:]
    k = k_ref[0]
    v = v_ref[0]
    lse_columns = lse_ref[0].T
    delta_columns = delta_ref[0].T
    dk = dv = None
    for first in range(0, groups, TOGETHER):
        members = range(first, first + TOGETHER)

        def rows(ref):
            return jnp.concatenate([ref[0, :, i * HEAD_SIZE : (i + 1) * HEAD_SIZE] for i in members], axis=0)

        def column(values):
            return jnp.concatenate([values[:, i : i + 1] for i in members], axis=0)

        q = rows(q_ref)
        g = rows(g_ref)
        w = jnp.exp2(dot_nt(q, k) * (SCALE * LOG2E) - column(lse_columns))
        ds = (w * (dot_nt(g, v) - column(delta_columns))).astype(jnp.bfloat16)
        dq = dot_nn(ds, k) * SCALE
        part_k = dot_tn(q, ds)
        part_v = dot_tn(g, w.astype(jnp.bfloat16))
        dk = part_k if dk is None else dk + part_k
        dv = part_v if dv is None else dv + part_v
        for i in members:
            start = (i - first) * dq_ref.shape[0]
            dq_ref[:, i * HEAD_SIZE : (i + 1) * HEAD_SIZE] = dq[start : start + dq_ref.shape[0]]
    dkv_ref[0] = (dk * SCALE).T.astype(jnp.bfloat16)
    dkv_ref[1] = dv.T.astype(jnp.bfloat16)


def row_spec(rows, groups):
    return pl.BlockSpec((1, rows.shape[1], groups * HEAD_SIZE), lambda h, at: (at[1], 0, h))


def image_specs(image_kv, heads):
    tokens = image_kv.shape[1]
    return [
        pl.BlockSpec((1, tokens, HEAD_SIZE), lambda h, at: (0, 0, at[0] * heads + h)),
        pl.BlockSpec((1, tokens, HEAD_SIZE), lambda h, at: (1, 0, at[0] * heads + h)),
    ]


def stat_spec(groups, text):
    return pl.BlockSpec((1, groups, text), lambda h, *at: (h, 0, 0))


def forward_call(at, q, image_kv, groups, heads):
    text = q.shape[1]
    width = groups * HEAD_SIZE
    tokens = image_kv.shape[1]
    lanes = groups * text
    return pl.pallas_call(
        functools.partial(forward_kernel, groups),
        grid_spec=pltpu.PrefetchScalarGridSpec(
            num_scalar_prefetch=1,
            grid=(heads,),
            in_specs=[row_spec(q, groups)] + image_specs(image_kv, heads),
            out_specs=[
                pl.BlockSpec((text, width), lambda h, at: (0, h)),
                pl.BlockSpec((1, HEAD_SIZE, lanes), lambda h, at: (h, 0, 0)),
                stat_spec(groups, text),
            ],
            scratch_shapes=[pltpu.VMEM((tokens + (-tokens) % 8, lanes), jnp.float32)],
        ),
        out_shape=[
            jax.ShapeDtypeStruct((text, heads * width), jnp.bfloat16),
            jax.ShapeDtypeStruct((heads, HEAD_SIZE, lanes), jnp.float32),
            jax.ShapeDtypeStruct((heads, groups, text), jnp.float32),
        ],
        compiler_params=params(),
        cost_estimate=pl.CostEstimate(
            flops=heads * 8 * tokens * lanes * HEAD_SIZE,
            bytes_accessed=heads * tokens * HEAD_SIZE * 4,
            transcendentals=heads * tokens * lanes,
        ),
        name="forward_group",
    )(at, q, image_kv, image_kv)


def delta_call(at, g, wide, groups, heads):
    text = g.shape[1]
    lanes = groups * text
    return pl.pallas_call(
        functools.partial(delta_kernel, groups),
        grid_spec=pltpu.PrefetchScalarGridSpec(
            num_scalar_prefetch=1,
            grid=(heads,),
            in_specs=[row_spec(g, groups), pl.BlockSpec((1, HEAD_SIZE, lanes), lambda h, at: (h, 0, 0))],
            out_specs=stat_spec(groups, text),
        ),
        out_shape=jax.ShapeDtypeStruct((heads, groups, text), jnp.float32),
        compiler_params=params(),
        cost_estimate=pl.CostEstimate(
            flops=heads * 2 * lanes * HEAD_SIZE, bytes_accessed=heads * lanes * HEAD_SIZE * 6, transcendentals=0
        ),
        name="delta_group",
    )(at, g, wide)


def backward_call(at, q, g, image_kv, lse, delta, grads, groups, heads):
    text = q.shape[1]
    width = groups * HEAD_SIZE
    tokens = image_kv.shape[1]
    lanes = groups * text
    stat = stat_spec(groups, text)
    in_specs = [row_spec(q, groups), row_spec(g, groups)] + image_specs(image_kv, heads) + [stat, stat]
    operands = [at, q, g, image_kv, image_kv, lse, delta]
    aliases = {}
    if grads is not None:
        in_specs.append(pl.BlockSpec(memory_space=pl.ANY))
        aliases = {len(operands): 1}
        operands.append(grads)
    return pl.pallas_call(
        functools.partial(backward_kernel, groups),
        grid_spec=pltpu.PrefetchScalarGridSpec(
            num_scalar_prefetch=1,
            grid=(heads,),
            in_specs=in_specs,
            out_specs=[
                pl.BlockSpec((text, width), lambda h, at: (0, h)),
                pl.BlockSpec((2, tokens, HEAD_SIZE), lambda h, at: (0, 0, at[0] * heads + h)),
            ],
        ),
        out_shape=[
            jax.ShapeDtypeStruct((text, heads * width), jnp.float32),
            jax.ShapeDtypeStruct(image_kv.shape, jnp.bfloat16),
        ],
        input_output_aliases=aliases,
        compiler_params=params(),
        cost_estimate=pl.CostEstimate(
            flops=heads * 20 * tokens * lanes * HEAD_SIZE,
            bytes_accessed=heads * tokens * HEAD_SIZE * 8,
            transcendentals=heads * tokens * lanes,
        ),
        name="backward_group",
    )(*operands)


def mix_kernel(groups, o_ref, own_ref, old_ref, carried_ref, out_ref):
    own = own_ref[0].T
    old = old_ref[0].T
    for i in range(groups):
        span = slice(i * HEAD_SIZE, (i + 1) * HEAD_SIZE)
        mix = o_ref[:, span].astype(jnp.float32) * own[:, i : i + 1]
        mix = mix + carried_ref[:, span].astype(jnp.float32) * old[:, i : i + 1]
        out_ref[:, span] = mix.astype(jnp.bfloat16)


def mix_call(out, own, old, carried):
    heads, groups, text = own.shape
    width = groups * HEAD_SIZE
    rows = pl.BlockSpec((text, width), lambda h: (0, h))
    return pl.pallas_call(
        functools.partial(mix_kernel, groups),
        grid=(heads,),
        in_specs=[rows, stat_spec(groups, text), stat_spec(groups, text), rows],
        out_specs=rows,
        out_shape=jax.ShapeDtypeStruct((text, heads * width), jnp.bfloat16),
        compiler_params=params(),
        cost_estimate=pl.CostEstimate(
            flops=4 * text * heads * width, bytes_accessed=6 * text * heads * width, transcendentals=0
        ),
        name="mix_group",
    )(out, own, old, carried)


def merged(lse, delta):
    top = jnp.max(lse, axis=0)
    share = jnp.exp2(lse - top)
    total = jnp.sum(share, axis=0)
    return top + jnp.log2(total), jnp.sum(share * delta, axis=0) / total


def shards(queries, image_key_value, image_spans, tile_counts, cross_gate, grad_out):
    seq_index = lax.axis_index("seq")
    seq_total = lax.axis_size("seq")
    enc_index = lax.axis_index("enc")
    enc_total = lax.axis_size("enc")
    text, width = queries.shape
    heads = image_key_value.shape[3] // (enc_total * HEAD_SIZE)
    groups = width // (heads * HEAD_SIZE)
    row_images = enc_total // TILES
    gate = jnp.tanh(cross_gate[0])
    steps = range(enc_total)

    spans = lax.dynamic_slice_in_dim(image_spans, seq_index * row_images, row_images, 0)
    offsets = spans[:, 0] - seq_index * text
    slots = jnp.arange(text, dtype=jnp.int32)
    in_own = slots[None, :] >= offsets[:, None]
    positions = jnp.where(in_own, seq_index * text, (seq_index + 1) * text) + slots[None, :]
    seen = (positions >= spans[:, :1]) & (positions < spans[:, 1:])

    sources = [lax.rem(enc_index - step + enc_total, enc_total) for step in steps]
    places = [source // TILES for source in sources]
    ats = [jnp.stack([source, places[0]]).astype(jnp.int32) for source in sources]
    counts = lax.dynamic_slice_in_dim(tile_counts, seq_index * row_images, row_images, 0)

    def of_place(x):
        return x[0] if row_images == 1 else lax.dynamic_index_in_dim(x, places[0], 0, False)

    def of_group(x, step):
        return lax.dynamic_index_in_dim(x, sources[step], 0, False)

    def placed(message, carried):
        if row_images == 1:
            return message
        base = jnp.zeros((row_images,) + message.shape, message.dtype) if carried is None else carried
        return lax.dynamic_update_index_in_dim(base, message, places[0], 0)

    in_use = (enc_index - places[0] * TILES) < of_place(counts)
    my_seen = of_place(seen) & in_use
    wide_own = in_own[:, None, None, None, :]
    order = jnp.stack(sources)

    def window(own, later):
        return jnp.where(in_own[:, :, None], own[None], later[None])

    middle = width // 2
    q_left, grad_out = lax.optimization_barrier((shifted(queries[:, :middle], "seq", -1), grad_out))
    q_later = jnp.concatenate([q_left, shifted(queries[:, middle:], "seq", -1)], axis=1)
    q_moving = window(queries, q_later)
    grad_mixed = (gate * grad_out.astype(jnp.float32)).astype(jnp.bfloat16)
    q_first, g_later, image_kv = lax.optimization_barrier(
        (q_moving, shifted(grad_mixed, "seq", -1), image_key_value)
    )
    q_rings = [q_first]
    g_rings = [window(grad_mixed, g_later)]
    image_kv = image_kv[:, 0]
    outs, wides, lse_ring, delta_ring = [], [], [], []
    for step in steps:
        more = step + 1 < enc_total
        if more:
            q_next = rotated(q_moving if step == 0 else q_rings[step], "enc", 1)
            if step == 0:
                q_next, image_kv = lax.optimization_barrier((q_next, image_kv))
            q_rings.append(q_next)
        out, wide, lse = forward_call(ats[step], q_rings[step], image_kv, groups, heads)
        outs.append(out)
        wides.append(wide)
        if step > 0:
            g_next, lse = lax.optimization_barrier((g_next, lse))
            g_rings.append(g_next)
        lse_ring.append(lse)
        if more:
            g_next = rotated(g_rings[step], "enc", 1)
        delta_ring.append(delta_call(ats[step], g_rings[step], wides[step], groups, heads))

    lse_mine = jnp.take(jnp.where(my_seen, jnp.stack(lse_ring), LOW), order, axis=0)
    delta_mine = jnp.take(jnp.stack(delta_ring), order, axis=0)
    mine = jnp.stack([lse_mine, delta_mine])
    early = row_images == 1
    tiles = [mine] + [rotated(mine, "enc", step) for step in steps[1:]]
    tile_lse = jnp.stack([t[0] for t in tiles])
    tile_delta = jnp.stack([t[1] for t in tiles])
    if early:
        first_out, tile_lse = lax.optimization_barrier((outs[1], tile_lse))
        mix_carried = rotated(first_out, "enc", 1)
    image_lse, image_delta = [], []
    for a in range(row_images):
        lse_a = tile_lse
        if row_images > 1:
            lse_a = jnp.where((jnp.stack(places) == a)[:, None, None, None, None], lse_a, LOW)
        lse_a, delta_a = merged(lse_a, tile_delta)
        image_lse.append(lse_a)
        image_delta.append(delta_a)
    image_lse, image_delta = jnp.stack(image_lse), jnp.stack(image_delta)
    upper = merged(jnp.where(wide_own, image_lse, LOW), image_delta)
    lower = merged(jnp.where(wide_own, LOW, image_lse), image_delta)
    lower, upper = lax.optimization_barrier((jnp.stack(lower), jnp.stack(upper)))
    from_before = shifted(lower, "seq", 1)
    from_after = shifted(upper, "seq", -1)
    if early:
        from_before, from_after, mix_carried = lax.optimization_barrier((from_before, from_after, mix_carried))
    before_lse = jnp.where(seq_index > 0, from_before[0], LOW)
    after_lse = jnp.where(seq_index < seq_total - 1, from_after[0], LOW)
    own_total = merged(jnp.stack([upper[0], before_lse]), jnp.stack([upper[1], from_before[1]]))
    next_total = merged(jnp.stack([lower[0], after_lse]), jnp.stack([lower[1], from_after[1]]))
    full_lse = jnp.where(wide_own, own_total[0], next_total[0])
    full_delta = jnp.where(wide_own, own_total[1], next_total[1])
    mine_share = jnp.where(my_seen, jnp.exp2(lse_mine - of_place(image_lse)), 0.0)
    home_share = jnp.where(full_lse > LOW / 2, jnp.exp2(image_lse - full_lse), 0.0) * gate
    lse_used = jnp.where(my_seen, of_place(full_lse), HIGH)
    delta_used = of_place(full_delta)

    def mixed(step, carried):
        share = of_group(mine_share, step)
        if carried is None:
            return mix_call(outs[step], share, share, jnp.zeros((text, width), jnp.bfloat16))
        old = jnp.ones_like(share)
        if early and step == 2:
            old = jnp.exp2(of_group(tile_lse[1], step) - of_group(of_place(image_lse), step))
        if early and step == 0:
            home = of_group(home_share[0], 0)
            share, old = share * home, old * home
        return mix_call(outs[step], share, old, of_place(carried) if row_images > 1 else carried)

    def homing(sums):
        sums = sums.reshape(row_images, text, width).astype(jnp.float32)
        kept = jnp.sum(jnp.where(in_own[:, :, None], sums, 0.0), axis=0)
        passed = jnp.sum(jnp.where(in_own[:, :, None], 0.0, sums), axis=0).astype(jnp.bfloat16)
        return kept, shifted(passed, "seq", 1)

    def homed(kept, passed):
        return (kept + passed.astype(jnp.float32)).astype(jnp.bfloat16)

    def scaled_home(sums):
        if early:
            return sums
        shares = jnp.stack([of_group(home_share[a], 0) for a in range(row_images)])
        shares = shares.reshape(row_images, heads * groups, text).transpose(0, 2, 1)
        parts = sums.reshape(row_images, text, heads * groups, HEAD_SIZE).astype(jnp.float32)
        return (parts * shares[..., None]).reshape(row_images, text, width).astype(jnp.bfloat16)

    if not early:
        mix_carried = rotated(placed(mixed(1, None), None), "enc", 1)
    mix_carried = placed(mixed(2, mix_carried), mix_carried)
    mix_moving = rotated(mix_carried, "enc", 1)
    grads = None
    carried = None
    for step in list(steps[1:]) + [0]:
        q = q_rings[step]
        grad_q, grads = backward_call(
            ats[step], q, g_rings[step], image_kv, of_group(lse_used, step), of_group(delta_used, step),
            grads, groups, heads,
        )
        if step == 0:
            grad_q, mix_passed = lax.optimization_barrier((grad_q, mix_passed))
        if carried is not None:
            grad_q = grad_q + (carried if row_images == 1 else of_place(carried)).astype(jnp.float32)
        carried = placed(grad_q.astype(jnp.bfloat16), carried)
        if step > 0:
            carried = rotated(carried, "enc", 1)
        if 0 < step < enc_total - 1:
            following = (step + 2) % enc_total
            if following == 0:
                continue
            mix_moving, grads = lax.optimization_barrier((mix_moving, grads))
            mix_carried = placed(mixed(following, mix_moving), mix_moving)
            mix_moving = rotated(mix_carried, "enc", 1)
        elif step > 0:
            mix_moving, grads = lax.optimization_barrier((mix_moving, grads))
            mix_carried = placed(mixed(0, mix_moving), mix_moving)
            mix_kept, mix_passed = homing(scaled_home(mix_carried))
    grads = join_pairs(grads).transpose(1, 0, 2).reshape(image_key_value.shape)

    grad_kept, grad_passed = homing(carried)
    return (homed(mix_kept, mix_passed), homed(grad_kept, grad_passed), grads)


def solution(mesh):
    in_specs = (
        P("seq", "enc"),
        P(None, ("seq", "enc"), None, None),
        P(),
        P(),
        P(),
        P("seq", "enc"),
    )
    out_specs = (P("seq", "enc"), P("seq", "enc"), P(None, ("seq", "enc"), None, None))
    return jax.shard_map(shards, mesh=mesh, in_specs=in_specs, out_specs=out_specs, check_vma=False)
```

```python
import functools

import jax
import jax.numpy as jnp
from jax import lax
from jax.experimental import pallas as pl
from jax.experimental.pallas import tpu as pltpu
from jax.sharding import PartitionSpec as P

HEAD_SIZE = 128
TILES = 4
LOW = -1e30
HIGH = 1e30
SCALE = HEAD_SIZE ** (-0.5)
LOG2E = 1.4426950408889634
PAIR_ROWS = 256
TOGETHER = 4


def rotated(x, axis, by):
    total = lax.axis_size(axis)
    return lax.ppermute(x, axis, [(i, (i + by) % total) for i in range(total)])


def shifted(x, axis, by):
    total = lax.axis_size(axis)
    return lax.ppermute(x, axis, [(i, i + by) for i in range(total) if 0 <= i + by < total])


def dot_nt(a, b):
    return lax.dot_general(a, b, (((1,), (1,)), ((), ())), preferred_element_type=jnp.float32)


def dot_tn(a, b):
    return lax.dot_general(a, b, (((0,), (0,)), ((), ())), preferred_element_type=jnp.float32)


def dot_nn(a, b):
    return lax.dot_general(a, b, (((1,), (0,)), ((), ())), preferred_element_type=jnp.float32)


def stacked(ref, groups):
    return jnp.concatenate(
        [ref[0, :, i * HEAD_SIZE : (i + 1) * HEAD_SIZE] for i in range(groups)], axis=0
    )


def params():
    return pltpu.CompilerParams(vmem_limit_bytes=48 * 1024 * 1024)


def join_kernel(x_ref, o_ref):
    o_ref[:, 0, :] = x_ref[0]
    o_ref[:, 1, :] = x_ref[1]


def join_pairs(halves):
    _, tokens, width = halves.shape
    return pl.pallas_call(
        join_kernel,
        grid=(pl.cdiv(tokens, PAIR_ROWS),),
        in_specs=[pl.BlockSpec((2, PAIR_ROWS, width), lambda i: (0, i, 0))],
        out_specs=pl.BlockSpec((PAIR_ROWS, 2, width), lambda i: (i, 0, 0)),
        out_shape=jax.ShapeDtypeStruct((tokens, 2, width), halves.dtype),
        compiler_params=pltpu.CompilerParams(vmem_limit_bytes=16 * 1024 * 1024),
        cost_estimate=pl.CostEstimate(
            flops=0, bytes_accessed=4 * tokens * width * 4, transcendentals=0
        ),
        name="join_pairs",
    )(halves)


def forward_kernel(groups, at_ref, q_ref, k_ref, v_ref, o_ref, wide_ref, lse_ref, s_ref):
    s = dot_nt(k_ref[0], stacked(q_ref, groups))
    s_ref[...] = s
    top = jnp.max(s, axis=0, keepdims=True) * (SCALE * LOG2E)
    p = jnp.exp2(s_ref[...] * (SCALE * LOG2E) - top)
    total = jnp.sum(p, axis=0, keepdims=True)
    out = dot_tn(v_ref[0], p.astype(jnp.bfloat16)) / total
    lse = top + jnp.log2(total)
    wide_ref[0] = out
    for i in range(groups):
        span = slice(i * HEAD_SIZE, (i + 1) * HEAD_SIZE)
        o_ref[:, span] = out[:, span].T.astype(jnp.bfloat16)
        lse_ref[0, i : i + 1] = lse[:, span]


def delta_kernel(groups, at_ref, g_ref, wide_ref, delta_ref):
    for i in range(groups):
        span = slice(i * HEAD_SIZE, (i + 1) * HEAD_SIZE)
        g_t = g_ref[0, :, span].astype(jnp.float32).T
        delta_ref[0, i : i + 1] = jnp.sum(g_t * wide_ref[0, :, span], axis=0, keepdims=True)


def backward_kernel(groups, at_ref, q_ref, g_ref, k_ref, v_ref, lse_ref, delta_ref, *rest):
    dq_ref, dkv_ref = rest[-2:]
    k = k_ref[0]
    v = v_ref[0]
    lse_columns = lse_ref[0].T
    delta_columns = delta_ref[0].T
    dk = dv = None
    for first in range(0, groups, TOGETHER):
        members = range(first, first + TOGETHER)

        def rows(ref):
            return jnp.concatenate([ref[0, :, i * HEAD_SIZE : (i + 1) * HEAD_SIZE] for i in members], axis=0)

        def column(values):
            return jnp.concatenate([values[:, i : i + 1] for i in members], axis=0)

        q = rows(q_ref)
        g = rows(g_ref)
        w = jnp.exp2(dot_nt(q, k) * (SCALE * LOG2E) - column(lse_columns))
        ds = (w * (dot_nt(g, v) - column(delta_columns))).astype(jnp.bfloat16)
        dq = dot_nn(ds, k) * SCALE
        part_k = dot_tn(q, ds)
        part_v = dot_tn(g, w.astype(jnp.bfloat16))
        dk = part_k if dk is None else dk + part_k
        dv = part_v if dv is None else dv + part_v
        for i in members:
            start = (i - first) * dq_ref.shape[0]
            dq_ref[:, i * HEAD_SIZE : (i + 1) * HEAD_SIZE] = dq[start : start + dq_ref.shape[0]]
    dkv_ref[0] = (dk * SCALE).T.astype(jnp.bfloat16)
    dkv_ref[1] = dv.T.astype(jnp.bfloat16)


def row_spec(rows, groups):
    return pl.BlockSpec((1, rows.shape[1], groups * HEAD_SIZE), lambda h, at: (at[1], 0, h))


def image_specs(image_kv, heads):
    tokens = image_kv.shape[1]
    return [
        pl.BlockSpec((1, tokens, HEAD_SIZE), lambda h, at: (0, 0, at[0] * heads + h)),
        pl.BlockSpec((1, tokens, HEAD_SIZE), lambda h, at: (1, 0, at[0] * heads + h)),
    ]


def stat_spec(groups, text):
    return pl.BlockSpec((1, groups, text), lambda h, *at: (h, 0, 0))


def forward_call(at, q, image_kv, groups, heads):
    text = q.shape[1]
    width = groups * HEAD_SIZE
    tokens = image_kv.shape[1]
    lanes = groups * text
    return pl.pallas_call(
        functools.partial(forward_kernel, groups),
        grid_spec=pltpu.PrefetchScalarGridSpec(
            num_scalar_prefetch=1,
            grid=(heads,),
            in_specs=[row_spec(q, groups)] + image_specs(image_kv, heads),
            out_specs=[
                pl.BlockSpec((text, width), lambda h, at: (0, h)),
                pl.BlockSpec((1, HEAD_SIZE, lanes), lambda h, at: (h, 0, 0)),
                stat_spec(groups, text),
            ],
            scratch_shapes=[pltpu.VMEM((tokens, lanes), jnp.float32)],
        ),
        out_shape=[
            jax.ShapeDtypeStruct((text, heads * width), jnp.bfloat16),
            jax.ShapeDtypeStruct((heads, HEAD_SIZE, lanes), jnp.float32),
            jax.ShapeDtypeStruct((heads, groups, text), jnp.float32),
        ],
        compiler_params=params(),
        cost_estimate=pl.CostEstimate(
            flops=heads * 8 * tokens * lanes * HEAD_SIZE,
            bytes_accessed=heads * tokens * HEAD_SIZE * 4,
            transcendentals=heads * tokens * lanes,
        ),
        name="forward_group",
    )(at, q, image_kv, image_kv)


def delta_call(at, g, wide, groups, heads):
    text = g.shape[1]
    lanes = groups * text
    return pl.pallas_call(
        functools.partial(delta_kernel, groups),
        grid_spec=pltpu.PrefetchScalarGridSpec(
            num_scalar_prefetch=1,
            grid=(heads,),
            in_specs=[row_spec(g, groups), pl.BlockSpec((1, HEAD_SIZE, lanes), lambda h, at: (h, 0, 0))],
            out_specs=stat_spec(groups, text),
        ),
        out_shape=jax.ShapeDtypeStruct((heads, groups, text), jnp.float32),
        compiler_params=params(),
        cost_estimate=pl.CostEstimate(
            flops=heads * 2 * lanes * HEAD_SIZE, bytes_accessed=heads * lanes * HEAD_SIZE * 6, transcendentals=0
        ),
        name="delta_group",
    )(at, g, wide)


def backward_call(at, q, g, image_kv, lse, delta, grads, groups, heads):
    text = q.shape[1]
    width = groups * HEAD_SIZE
    tokens = image_kv.shape[1]
    lanes = groups * text
    stat = stat_spec(groups, text)
    in_specs = [row_spec(q, groups), row_spec(g, groups)] + image_specs(image_kv, heads) + [stat, stat]
    operands = [at, q, g, image_kv, image_kv, lse, delta]
    aliases = {}
    if grads is not None:
        in_specs.append(pl.BlockSpec(memory_space=pl.ANY))
        aliases = {len(operands): 1}
        operands.append(grads)
    return pl.pallas_call(
        functools.partial(backward_kernel, groups),
        grid_spec=pltpu.PrefetchScalarGridSpec(
            num_scalar_prefetch=1,
            grid=(heads,),
            in_specs=in_specs,
            out_specs=[
                pl.BlockSpec((text, width), lambda h, at: (0, h)),
                pl.BlockSpec((2, tokens, HEAD_SIZE), lambda h, at: (0, 0, at[0] * heads + h)),
            ],
        ),
        out_shape=[
            jax.ShapeDtypeStruct((text, heads * width), jnp.float32),
            jax.ShapeDtypeStruct(image_kv.shape, jnp.bfloat16),
        ],
        input_output_aliases=aliases,
        compiler_params=params(),
        cost_estimate=pl.CostEstimate(
            flops=heads * 20 * tokens * lanes * HEAD_SIZE,
            bytes_accessed=heads * tokens * HEAD_SIZE * 8,
            transcendentals=heads * tokens * lanes,
        ),
        name="backward_group",
    )(*operands)


def mix_kernel(groups, o_ref, own_ref, old_ref, carried_ref, out_ref):
    own = own_ref[0].T
    old = old_ref[0].T
    for i in range(groups):
        span = slice(i * HEAD_SIZE, (i + 1) * HEAD_SIZE)
        mix = o_ref[:, span].astype(jnp.float32) * own[:, i : i + 1]
        mix = mix + carried_ref[:, span].astype(jnp.float32) * old[:, i : i + 1]
        out_ref[:, span] = mix.astype(jnp.bfloat16)


def mix_call(out, own, old, carried):
    heads, groups, text = own.shape
    width = groups * HEAD_SIZE
    rows = pl.BlockSpec((text, width), lambda h: (0, h))
    return pl.pallas_call(
        functools.partial(mix_kernel, groups),
        grid=(heads,),
        in_specs=[rows, stat_spec(groups, text), stat_spec(groups, text), rows],
        out_specs=rows,
        out_shape=jax.ShapeDtypeStruct((text, heads * width), jnp.bfloat16),
        compiler_params=params(),
        cost_estimate=pl.CostEstimate(
            flops=4 * text * heads * width, bytes_accessed=6 * text * heads * width, transcendentals=0
        ),
        name="mix_group",
    )(out, own, old, carried)


def merged(lse, delta):
    top = jnp.max(lse, axis=0)
    share = jnp.exp2(lse - top)
    total = jnp.sum(share, axis=0)
    return top + jnp.log2(total), jnp.sum(share * delta, axis=0) / total


def shards(queries, image_key_value, image_spans, tile_counts, cross_gate, grad_out):
    seq_index = lax.axis_index("seq")
    seq_total = lax.axis_size("seq")
    enc_index = lax.axis_index("enc")
    enc_total = lax.axis_size("enc")
    text, width = queries.shape
    heads = image_key_value.shape[3] // (enc_total * HEAD_SIZE)
    groups = width // (heads * HEAD_SIZE)
    row_images = enc_total // TILES
    gate = jnp.tanh(cross_gate[0])
    steps = range(enc_total)

    spans = lax.dynamic_slice_in_dim(image_spans, seq_index * row_images, row_images, 0)
    offsets = spans[:, 0] - seq_index * text
    slots = jnp.arange(text, dtype=jnp.int32)
    in_own = slots[None, :] >= offsets[:, None]
    positions = jnp.where(in_own, seq_index * text, (seq_index + 1) * text) + slots[None, :]
    seen = (positions >= spans[:, :1]) & (positions < spans[:, 1:])

    sources = [lax.rem(enc_index - step + enc_total, enc_total) for step in steps]
    places = [source // TILES for source in sources]
    ats = [jnp.stack([source, places[0]]).astype(jnp.int32) for source in sources]
    counts = lax.dynamic_slice_in_dim(tile_counts, seq_index * row_images, row_images, 0)

    def of_place(x):
        return x[0] if row_images == 1 else lax.dynamic_index_in_dim(x, places[0], 0, False)

    def of_group(x, step):
        return lax.dynamic_index_in_dim(x, sources[step], 0, False)

    def placed(message, carried):
        if row_images == 1:
            return message
        base = jnp.zeros((row_images,) + message.shape, message.dtype) if carried is None else carried
        return lax.dynamic_update_index_in_dim(base, message, places[0], 0)

    in_use = (enc_index - places[0] * TILES) < of_place(counts)
    my_seen = of_place(seen) & in_use
    wide_own = in_own[:, None, None, None, :]
    order = jnp.stack(sources)

    def window(own, later):
        return jnp.where(in_own[:, :, None], own[None], later[None])

    middle = width // 2
    q_left, grad_out = lax.optimization_barrier((shifted(queries[:, :middle], "seq", -1), grad_out))
    q_later = jnp.concatenate([q_left, shifted(queries[:, middle:], "seq", -1)], axis=1)
    q_moving = window(queries, q_later)
    grad_mixed = (gate * grad_out.astype(jnp.float32)).astype(jnp.bfloat16)
    q_first, g_later, image_kv = lax.optimization_barrier(
        (q_moving, shifted(grad_mixed, "seq", -1), image_key_value)
    )
    q_rings = [q_first]
    g_rings = [window(grad_mixed, g_later)]
    image_kv = image_kv[:, 0]
    outs, wides, lse_ring, delta_ring = [], [], [], []
    for step in steps:
        more = step + 1 < enc_total
        if more:
            q_next = rotated(q_moving if step == 0 else q_rings[step], "enc", 1)
            if step == 0:
                q_next, image_kv = lax.optimization_barrier((q_next, image_kv))
            q_rings.append(q_next)
        out, wide, lse = forward_call(ats[step], q_rings[step], image_kv, groups, heads)
        outs.append(out)
        wides.append(wide)
        if step > 0:
            g_next, lse = lax.optimization_barrier((g_next, lse))
            g_rings.append(g_next)
        lse_ring.append(lse)
        if more:
            g_next = rotated(g_rings[step], "enc", 1)
        delta_ring.append(delta_call(ats[step], g_rings[step], wides[step], groups, heads))

    lse_mine = jnp.take(jnp.where(my_seen, jnp.stack(lse_ring), LOW), order, axis=0)
    delta_mine = jnp.take(jnp.stack(delta_ring), order, axis=0)
    mine = jnp.stack([lse_mine, delta_mine])
    early = row_images == 1
    tiles = [mine] + [rotated(mine, "enc", step) for step in steps[1:]]
    tile_lse = jnp.stack([t[0] for t in tiles])
    tile_delta = jnp.stack([t[1] for t in tiles])
    if early:
        first_out, tile_lse = lax.optimization_barrier((outs[1], tile_lse))
        mix_carried = rotated(first_out, "enc", 1)
    image_lse, image_delta = [], []
    for a in range(row_images):
        lse_a = tile_lse
        if row_images > 1:
            lse_a = jnp.where((jnp.stack(places) == a)[:, None, None, None, None], lse_a, LOW)
        lse_a, delta_a = merged(lse_a, tile_delta)
        image_lse.append(lse_a)
        image_delta.append(delta_a)
    image_lse, image_delta = jnp.stack(image_lse), jnp.stack(image_delta)
    upper = merged(jnp.where(wide_own, image_lse, LOW), image_delta)
    lower = merged(jnp.where(wide_own, LOW, image_lse), image_delta)
    lower, upper = lax.optimization_barrier((jnp.stack(lower), jnp.stack(upper)))
    from_before = shifted(lower, "seq", 1)
    from_after = shifted(upper, "seq", -1)
    if early:
        from_before, from_after, mix_carried = lax.optimization_barrier((from_before, from_after, mix_carried))
    before_lse = jnp.where(seq_index > 0, from_before[0], LOW)
    after_lse = jnp.where(seq_index < seq_total - 1, from_after[0], LOW)
    own_total = merged(jnp.stack([upper[0], before_lse]), jnp.stack([upper[1], from_before[1]]))
    next_total = merged(jnp.stack([lower[0], after_lse]), jnp.stack([lower[1], from_after[1]]))
    full_lse = jnp.where(wide_own, own_total[0], next_total[0])
    full_delta = jnp.where(wide_own, own_total[1], next_total[1])
    mine_share = jnp.where(my_seen, jnp.exp2(lse_mine - of_place(image_lse)), 0.0)
    home_share = jnp.where(full_lse > LOW / 2, jnp.exp2(image_lse - full_lse), 0.0) * gate
    lse_used = jnp.where(my_seen, of_place(full_lse), HIGH)
    delta_used = of_place(full_delta)

    def mixed(step, carried):
        share = of_group(mine_share, step)
        if carried is None:
            return mix_call(outs[step], share, share, jnp.zeros((text, width), jnp.bfloat16))
        old = jnp.ones_like(share)
        if early and step == 2:
            old = jnp.exp2(of_group(tile_lse[1], step) - of_group(of_place(image_lse), step))
        if early and step == 0:
            home = of_group(home_share[0], 0)
            share, old = share * home, old * home
        return mix_call(outs[step], share, old, of_place(carried) if row_images > 1 else carried)

    def homing(sums):
        sums = sums.reshape(row_images, text, width).astype(jnp.float32)
        kept = jnp.sum(jnp.where(in_own[:, :, None], sums, 0.0), axis=0)
        passed = jnp.sum(jnp.where(in_own[:, :, None], 0.0, sums), axis=0).astype(jnp.bfloat16)
        return kept, shifted(passed, "seq", 1)

    def homed(kept, passed):
        return (kept + passed.astype(jnp.float32)).astype(jnp.bfloat16)

    def scaled_home(sums):
        if early:
            return sums
        shares = jnp.stack([of_group(home_share[a], 0) for a in range(row_images)])
        shares = shares.reshape(row_images, heads * groups, text).transpose(0, 2, 1)
        parts = sums.reshape(row_images, text, heads * groups, HEAD_SIZE).astype(jnp.float32)
        return (parts * shares[..., None]).reshape(row_images, text, width).astype(jnp.bfloat16)

    if not early:
        mix_carried = rotated(placed(mixed(1, None), None), "enc", 1)
    mix_carried = placed(mixed(2, mix_carried), mix_carried)
    mix_moving = rotated(mix_carried, "enc", 1)
    grads = None
    carried = None
    for step in list(steps[1:]) + [0]:
        q = q_rings[step]
        grad_q, grads = backward_call(
            ats[step], q, g_rings[step], image_kv, of_group(lse_used, step), of_group(delta_used, step),
            grads, groups, heads,
        )
        if step == 0:
            grad_q, mix_passed = lax.optimization_barrier((grad_q, mix_passed))
        if carried is not None:
            grad_q = grad_q + (carried if row_images == 1 else of_place(carried)).astype(jnp.float32)
        carried = placed(grad_q.astype(jnp.bfloat16), carried)
        if step > 0:
            carried = rotated(carried, "enc", 1)
        if 0 < step < enc_total - 1:
            following = (step + 2) % enc_total
            if following == 0:
                continue
            mix_moving, grads = lax.optimization_barrier((mix_moving, grads))
            mix_carried = placed(mixed(following, mix_moving), mix_moving)
            mix_moving = rotated(mix_carried, "enc", 1)
        elif step > 0:
            mix_moving, grads = lax.optimization_barrier((mix_moving, grads))
            mix_carried = placed(mixed(0, mix_moving), mix_moving)
            mix_kept, mix_passed = homing(scaled_home(mix_carried))
    grads = join_pairs(grads).transpose(1, 0, 2).reshape(image_key_value.shape)

    grad_kept, grad_passed = homing(carried)
    return (homed(mix_kept, mix_passed), homed(grad_kept, grad_passed), grads)


def solution(mesh):
    in_specs = (
        P("seq", "enc"),
        P(None, ("seq", "enc"), None, None),
        P(),
        P(),
        P(),
        P("seq", "enc"),
    )
    out_specs = (P("seq", "enc"), P("seq", "enc"), P(None, ("seq", "enc"), None, None))
    return jax.shard_map(shards, mesh=mesh, in_specs=in_specs, out_specs=out_specs, check_vma=False)
```
